32 devices in a mesh: energy: 16 (over z, x, core), slab: 2 (over y).
Axes of the slice: x: 2, y: 2, z: 4, core: 2. Of those that a mesh axis runs over, the one named last changes fastest.
Arguments:
- energies: float32 [16], P('energy'), may hold values from 0.6 to 1.2
- hamiltonian: float32 [2, 256, 256], P('slab')
- coupling: float32 [2, 64, 64], P('slab'), may hold values from -1.04 to 1.04
- green_prev: float32 [16, 2, 2, 256, 256], P('energy', 'slab'), may hold values from -0.5 to 0.5
- profile: float32 [256, 256], replicated, may hold values from 0.2 to 1
- phonon_weights: float32 [8], replicated, may hold values from 0.02 to 0.1
- source: int32 [16, 2], P('energy'), may hold values from 0 to 15, as said below
- weight_index: int32 [16, 2], P('energy'), may hold values from 0 to 7
- left_face: int32 [2, 64], P('slab'), may hold values from 0 to 255, as said below
- right_face: int32 [2, 64], P('slab'), may hold values from 0 to 255, as said below
Outputs:
- green: float32 [16, 2, 2, 256, 256], P('energy', 'slab')
The draws below stay inside these ranges and needn't reach their ends.
Inputs may be any that keep to these rules, and one draw needn't show every extreme that they name: source[j, 0] = min(j + d, 15) and source[j, 1] = max(j - d', 0) with d, d' in 1 .. 5; in each column some energy has its partner exactly 5 points away. `left_face`: each row holds 64 distinct orbitals. right_face[s] holds the same 64 orbitals as left_face[s], in an order of its own.
All inputs are finite; a program needn't handle non-finite values.
Results may differ from the reference program's by a relative error of at most 0.00011.
Values sent between devices are 32-bit elements; how exact they have to be, the bound alone decides.
No kernel may reach another device: no remote copies, remote signals or barrier semaphores. Data moves between devices by JAX's collectives and lax.ppermute only.
A program may use at most 64 MiB of HBM per device.

```python
import math
import jax
import jax.numpy as jnp
from jax import lax

W = 256
S = 64
SPAN = 5
NW = 8
NEWTON = 5
NE = 16
SLABS = 2


def draw_hamiltonian(key, part):
    key_a, key_b = jax.random.split(jax.random.fold_in(key, 5))
    raw = jax.random.normal(key_a, (SLABS, W, W), jnp.float32)
    onsite = jax.random.uniform(key_b, (SLABS, W), jnp.float32, -0.1, 0.1)
    scaled = raw * (0.1 * (2.0 / W) ** 0.5)
    symmetric = 0.5 * (scaled + jnp.swapaxes(scaled, 1, 2))
    return symmetric + onsite[:, :, None] * jnp.eye(W, dtype=jnp.float32)[None]


def draw_coupling(key, part):
    key_size, key_sign, key_noise = jax.random.split(jax.random.fold_in(key, 53), 3)
    signs = jnp.where(jax.random.bernoulli(key_sign, 0.5, (SLABS, S)), 1.0, -1.0).astype(jnp.float32)
    size = jax.random.uniform(key_size, (SLABS, S), jnp.float32, 0.75, 1.25)
    noise = jnp.clip(jax.random.normal(key_noise, (SLABS, S, S), jnp.float32), -3.0, 3.0)
    unit = jnp.eye(S, dtype=jnp.float32)
    off_part = noise * (1.0 - unit)[None] * (0.8 * 0.25 / S ** 0.5)
    return 0.8 * (signs * size)[:, :, None] * unit[None] + off_part


def draw_source(key, part):
    key_off, key_pos = jax.random.split(jax.random.fold_in(key, 11))
    offsets = jax.random.randint(key_off, (NE, 2), 1, SPAN + 1)
    spots = jax.random.randint(key_pos, (2,), SPAN, NE - SPAN)
    offsets = offsets.at[spots, jnp.arange(2)].set(SPAN)
    points = jnp.arange(NE, dtype=jnp.int32)
    upper = jnp.minimum(points + offsets[:, 0], NE - 1)
    lower = jnp.maximum(points - offsets[:, 1], 0)
    return jnp.stack([upper, lower], axis=1).astype(jnp.int32)


def face_indices(key):
    keys = jax.random.split(jax.random.fold_in(key, 21), SLABS)
    return jax.vmap(lambda item: jax.random.permutation(item, W)[:S])(keys).astype(jnp.int32)


def draw_left_face(key, part):
    return face_indices(key)


def draw_right_face(key, part):
    left = face_indices(key)
    keys = jax.random.split(jax.random.fold_in(key, 37), SLABS)
    order = jax.vmap(lambda item: jax.random.permutation(item, S))(keys).astype(jnp.int32)
    return jnp.take_along_axis(left, order, axis=1).astype(jnp.int32)


def place_ends(entries, key, least, largest):
    spot = [jax.random.randint(jax.random.fold_in(key, axis), (), 0, length) for axis, length in enumerate(entries.shape)]
    main_axis = entries.shape.index(max(entries.shape))
    next_to = spot[:main_axis] + [(spot[main_axis] + 1) % entries.shape[main_axis]] + spot[main_axis + 1:]
    return entries.at[tuple(spot)].set(least).at[tuple(next_to)].set(largest)


def levels(own_key, extent, shards, smallest, high):
    def one(position, blocks):
        draws = jax.random.uniform(jax.random.fold_in(jax.random.fold_in(own_key, 6), position), (blocks,), jnp.float32, smallest / len(shards), high / len(shards))
        return jnp.repeat(jnp.exp(draws), extent[position] // blocks).reshape((-1,) + (1,) * (len(extent) - position - 1))

    loudness = one(*shards[0])
    for cut in shards[1:]:
        loudness = loudness * one(*cut)
    return loudness


def bell_draw(own_key, shape, spread, bound, pieces=(), kind=jnp.bfloat16):
    entries = spread * jax.random.normal(own_key, shape, jnp.float32)
    if pieces:
        entries = entries * levels(own_key, shape, pieces, -0.22, 0.18)
    return jnp.clip(entries, -bound, bound).astype(kind)


def setup_inputs(seed: int = 0) -> dict:
    splits = jax.random.split(jax.random.key(seed), 11)
    return {
        "energies": jnp.clip(0.6 + 0.6 * jax.random.uniform(splits[0], (NE,), jnp.float32) ** levels(splits[0], (NE,), ((0, 16),), -0.2, 0.2), 0.6, 1.2),
        "hamiltonian": draw_hamiltonian(jax.random.fold_in(splits[10], 71), 0),
        "coupling": draw_coupling(jax.random.fold_in(splits[10], 71), 0),
        "green_prev": bell_draw(splits[3], (NE, SLABS, 2, W, W), (0.5 / W ** 0.5), 0.5, ((0, 16), (1, 2)), jnp.float32),
        "profile": jnp.clip(jax.random.uniform(splits[4], (W, W), jnp.float32, 0.2, 1.0), 0.2, 1.0),
        "phonon_weights": jnp.clip(jnp.exp(jax.random.uniform(splits[5], (NW,), jnp.float32, math.log(0.02), math.log(0.1))), 0.02, 0.1),
        "source": draw_source(jax.random.fold_in(splits[10], 71), 0),
        "weight_index": place_ends(jax.random.randint(splits[7], (NE, 2), 0, NW), jax.random.fold_in(splits[7], 1), 0, NW - 1).astype(jnp.int32),
        "left_face": draw_left_face(jax.random.fold_in(splits[10], 71), 0),
        "right_face": draw_right_face(jax.random.fold_in(splits[10], 71), 0),
    }


BROAD = 0.02
highest = lax.Precision.HIGHEST

def product(left, right):
    return jnp.matmul(left, right, precision=highest)

def complex_product(a_real, a_imag, b_real, b_imag):
    return (product(a_real, b_real) - product(a_imag, b_imag), product(a_real, b_imag) + product(a_imag, b_real))

def invert(a_real, a_imag):
    width = a_real.shape[-1]
    unit = jnp.eye(width, dtype=a_real.dtype)
    modulus = jnp.sqrt(a_real * a_real + a_imag * a_imag)
    col_norm = lax.optimization_barrier(jnp.max(lax.optimization_barrier(jnp.sum(modulus, axis=-2)), axis=-1))
    row_norm = lax.optimization_barrier(jnp.max(lax.optimization_barrier(jnp.sum(modulus, axis=-1)), axis=-1))
    scale = (1.0 / (col_norm * row_norm))[..., None, None]
    x_real = scale * jnp.swapaxes(a_real, -1, -2)
    x_imag = -scale * jnp.swapaxes(a_imag, -1, -2)
    for turn in range(NEWTON):
        p_real, p_imag = complex_product(a_real, a_imag, x_real, x_imag)
        x_real, x_imag = complex_product(x_real, x_imag, 2.0 * unit - p_real, -p_imag)
    return (x_real, x_imag)

def reference(energies, hamiltonian, coupling, green_prev, profile, phonon_weights, source, weight_index, left_face, right_face):
    width = hamiltonian.shape[1]
    unit = jnp.eye(width, dtype=hamiltonian.dtype)
    firsts = jnp.arange(SLABS) == 0

    def one_energy(items):
        energy, src, widx = items
        picked = green_prev[src]
        weights = phonon_weights[widx]
        sigma = profile * (weights[0] * picked[0] + weights[1] * picked[1])

        def forward(carry, slab):
            face_real, face_imag = carry
            ham, coup, sig, left, right, first = slab
            lead = -0.5 * product(coup.T, coup)
            inner_real = product(product(coup.T, face_real), coup)
            inner_imag = product(product(coup.T, face_imag), coup)
            b_real = jnp.where(first, 0.0, inner_real)
            b_imag = jnp.where(first, lead, inner_imag)
            a_real = energy * unit - ham - sig[0]
            a_imag = BROAD * unit - sig[1]
            a_real = a_real.at[left[:, None], left[None, :]].add(-b_real)
            a_imag = a_imag.at[left[:, None], left[None, :]].add(-b_imag)
            g_real, g_imag = invert(a_real, a_imag)
            out = (g_real[right][:, right], g_imag[right][:, right])
            return (out, (g_real, g_imag))
        zeros = jnp.zeros((S, S), hamiltonian.dtype)
        carry, (g_real, g_imag) = lax.scan(forward, (zeros, zeros), (hamiltonian, coupling, sigma, left_face, right_face, firsts))

        def backward(carry, slab):
            m_real, m_imag = carry
            gr_one, gi_one, coup, left, right = slab
            t_real, t_imag = complex_product(gr_one[:, right], gi_one[:, right], m_real, m_imag)
            c_real, c_imag = complex_product(t_real, t_imag, gr_one[right], gi_one[right])
            big_real = gr_one + c_real
            big_imag = gi_one + c_imag
            corner_real = big_real[left][:, left]
            corner_imag = big_imag[left][:, left]
            out = (product(product(coup, corner_real), coup.T), product(product(coup, corner_imag), coup.T))
            return (out, jnp.stack([big_real, big_imag], axis=0))
        carry, blocks = lax.scan(backward, (zeros, zeros), (g_real, g_imag, coupling, left_face, right_face), reverse=True)
        return blocks
    return lax.map(one_energy, (energies, source, weight_index))
```

```python
import jax
import jax.numpy as jnp
from jax import lax
from jax.experimental import pallas as pl
from jax.experimental.pallas import tpu as pltpu
from jax.sharding import PartitionSpec as P

SPAN = 5
BROAD = 0.02
DOUBLINGS = 4

f32 = jnp.float32
bf16 = jnp.bfloat16
NN = (((1,), (0,)), ((), ()))
NT = (((1,), (1,)), ((), ()))
TN = (((0,), (0,)), ((), ()))


def split(x):
    high = x.astype(bf16)
    return high, (x - high.astype(f32)).astype(bf16)


def mm(a, b, dims=NN):
    return lax.dot_general(a, b, dims, preferred_element_type=f32)


def left3(*terms):
    out = []
    for x in terms:
        high, low = split(x)
        out += [high, high, low]
    return jnp.concatenate(out, axis=1)


def right3(*terms, axis=0):
    out = []
    for x in terms:
        high, low = split(x)
        out += [high, low, high]
    return jnp.concatenate(out, axis=axis)


def pair(x, axis):
    return jnp.concatenate(split(x), axis=axis)


def twice(x, axis):
    return jnp.concatenate([x, x], axis=axis)


def both(x_re, x_im):
    return jnp.concatenate([x_re, x_im], axis=0)


def skew(e):
    return 0.5 * (e - e.T)


def herm_left(e, q):
    return left3(e, -2.0 * q)


def any_left(y_re, y_im):
    return jnp.concatenate([left3(y_re, -(y_re + y_im)), left3(y_im, y_re - y_im)], axis=0)


def complex_mm(a_re, a_im, b_re, b_im):
    rows = a_re.shape[0]
    out = mm(
        jnp.concatenate([left3(a_re, -a_im), left3(a_im, a_re)], axis=0), right3(b_re, b_im)
    )
    return out[:rows], out[rows:]


def one_hot(width, face):
    return (lax.broadcasted_iota(jnp.int32, (width, face.shape[1]), 0) == face).astype(bf16)


def unit_of(width):
    row = lax.broadcasted_iota(jnp.int32, (width, width), 0)
    return (row == lax.broadcasted_iota(jnp.int32, (width, width), 1)).astype(f32)


def assemble(energy, ham, profile, sig, coup, left, in_re, in_im):
    width, faces = ham.shape[0], coup.shape[0]
    placed = mm(twice(one_hot(width, left), 1), pair(coup, 1), NT)
    t_re = mm(left3(placed), right3(in_re))
    t_im = mm(left3(placed), right3(in_im))
    bound = mm(both(left3(t_re), left3(t_im)), right3(placed, axis=1), NT)
    unit = unit_of(width)
    a_re = energy * unit - ham - profile * sig[0] - bound[:width]
    a_im = BROAD * unit - profile * sig[1] - bound[width:]
    return a_re, a_im


def begin(a_re, a_im):
    total = a_re + a_im
    gram = mm(left3(total, -2.0 * a_re), right3(total, a_im, axis=1), NT)
    modulus = jnp.sqrt(a_re * a_re + a_im * a_im)
    col_norm = jnp.max(jnp.sum(modulus, axis=0))
    row_norm = jnp.max(jnp.sum(modulus, axis=1))
    scale = 1.0 / (col_norm * row_norm)
    e = unit_of(a_re.shape[0]) - scale * gram
    return e, (-scale) * skew(gram), scale


def corner(a_re, a_im, right):
    width, faces = a_re.shape[0], right.shape[1]
    hot = one_hot(width, right)
    e, q, scale = begin(a_re, a_im)
    picked = twice(hot.T, 1)
    y_re = scale * mm(picked, pair(a_re, 1), NT)
    y_im = -scale * mm(picked, pair(a_im, 1), NT)
    powers = []
    for turn in range(DOUBLINGS):
        powers.append((e, q))
        weights = right3(e, q)
        if turn < DOUBLINGS - 1:
            out = mm(jnp.concatenate([herm_left(e, q), any_left(y_re, y_im)], axis=0), weights)
            e = out[:width]
            q = skew(e)
            out = out[width:]
        else:
            out = mm(any_left(y_re, y_im), weights)
        y_re = y_re + out[:faces]
        y_im = y_im + out[faces:]
    out = mm(any_left(y_re, y_im), weights)
    out = mm(any_left(out[:faces], out[faces:]), weights)
    y_re = y_re + out[:faces]
    y_im = y_im + out[faces:]
    face = mm(pair(both(y_re, y_im), 1), twice(hot, 0))
    return face[:faces], face[faces:], powers, scale


def lead_face(faces):
    return jnp.zeros((faces, faces), f32), -0.5 * unit_of(faces)


def first_kernel(energy, ham, profile, sig, coup, left, right, face_out):
    faces = coup.shape[0]
    a_re, a_im = assemble(energy[0], ham[...], profile[...], sig, coup[...], left[...], *lead_face(faces))
    f_re, f_im, _, _ = corner(a_re, a_im, right[...])
    face_out[:, :faces] = f_re
    face_out[:, faces:] = f_im


def message_of(f_re, f_im, m_re, m_im, coup, left, right, width):
    faces = coup.shape[0]
    order = mm(one_hot(width, left), one_hot(width, right), TN).astype(bf16)
    mixed = mm(pair(coup, 1), twice(order, 0))
    if m_re is not None:
        t_re, t_im = complex_mm(f_re, f_im, m_re, m_im)
        c_re, c_im = complex_mm(t_re, t_im, f_re, f_im)
        f_re, f_im = f_re + c_re, f_im + c_im
    t = mm(left3(both(f_re, f_im)), right3(mixed, axis=1), NT)
    wide = jnp.concatenate([t[:faces], t[faces:]], axis=1)
    return mm(left3(mixed), right3(wide))


def next_kernel(
    energy, first, ham, profile, sig, coup, left, right, incoming,
    face_out, message_out, e_out, q_out, a_out, scale_out,
):
    width, faces = ham.shape[0], coup.shape[0]
    lead_re, lead_im = lead_face(faces)
    is_first = first[0] == 1
    in_re = jnp.where(is_first, lead_re, incoming[:, :faces])
    in_im = jnp.where(is_first, lead_im, incoming[:, faces:])
    a_re, a_im = assemble(energy[0], ham[...], profile[...], sig, coup[...], left[...], in_re, in_im)
    f_re, f_im, powers, scale = corner(a_re, a_im, right[...])
    face_out[:, :faces] = f_re
    face_out[:, faces:] = f_im
    message_out[...] = message_of(f_re, f_im, None, None, coup[...], left[...], right[...], width)
    for turn, (e, q) in enumerate(powers):
        e_out[turn] = e
        q_out[turn] = q
    a_out[0] = a_re
    a_out[1] = a_im
    scale_out[0] = scale


def message_kernel(face, message, coup, left, right, width_like, message_out):
    faces = coup.shape[0]
    message_out[...] = message_of(
        face[:, :faces], face[:, faces:], message[:, :faces], message[:, faces:],
        coup[...], left[...], right[...], width_like.shape[0],
    )


def full_kernel(scale, e_in, q_in, a_in, right, g_out, cols_out, rows_out):
    width, faces = a_in.shape[1], right.shape[1]
    unit = unit_of(width)
    s_e, s_q = unit + e_in[0], q_in[0]
    for turn in range(1, DOUBLINGS):
        e, q = e_in[turn], q_in[turn]
        weights = right3(e, q)
        if turn < DOUBLINGS - 1:
            s_e = s_e + mm(herm_left(s_e, s_q), weights)
        else:
            out = mm(jnp.concatenate([herm_left(s_e, s_q), herm_left(e, q)], axis=0), weights)
            s_e = s_e + out[:width]
            e = out[width:]
        s_q = skew(s_e)
    s_e = s_e + mm(herm_left(s_e, s_q), right3(e, skew(e)))
    s_q = skew(s_e)
    b, c = a_in[0].T, a_in[1].T
    g = scale[0] * mm(any_left(b, -c), right3(s_e, s_q))
    g_out[0] = g[:width]
    g_out[1] = g[width:]
    hot = one_hot(width, right[...])
    high, low = split(g)
    cols_out[...] = mm(jnp.concatenate([high, low], axis=1), twice(hot, 0))
    wide_high = jnp.concatenate([high[:width], high[width:]], axis=1)
    wide_low = jnp.concatenate([low[:width], low[width:]], axis=1)
    rows_out[...] = mm(twice(hot.T, 1), jnp.concatenate([wide_high, wide_low], axis=0))


def last_kernel(g, cols, rows, message, green_out):
    width, faces = g.shape[1], message.shape[0]
    t_re, t_im = complex_mm(
        message[:, :faces], message[:, faces:], rows[:, :width], rows[:, width:]
    )
    c_re, c_im = complex_mm(cols[:width], cols[width:], t_re, t_im)
    green_out[0, 0, 0] = g[0] + c_re
    green_out[0, 0, 1] = g[1] + c_im


def call(kernel, outs, scalars, *arrays, scalar_outs=()):
    smem = pl.BlockSpec(memory_space=pltpu.SMEM)
    vmem = pl.BlockSpec(memory_space=pltpu.VMEM)
    return pl.pallas_call(
        kernel,
        out_shape=[jax.ShapeDtypeStruct(shape, f32) for shape in (*outs, *scalar_outs)],
        in_specs=[smem] * len(scalars) + [vmem] * len(arrays),
        out_specs=[vmem] * len(outs) + [smem] * len(scalar_outs),
        compiler_params=pltpu.CompilerParams(vmem_limit_bytes=40 * 2**20),
    )(*scalars, *arrays)


def passed_along(value, axis, steps):
    count = lax.axis_size(axis)
    initial, last = (max(0, -steps), min(count, count - steps))
    return lax.ppermute(value, axis, [(source, source + steps) for source in range(initial, last)])


def exchange(green_prev, phonon_weights, source, weight_index):
    base = lax.axis_index("energy")
    table_size = phonon_weights.shape[0]
    chosen = jnp.sum(
        phonon_weights[None, :] * (weight_index[0][:, None] == jnp.arange(table_size, dtype=jnp.int32)[None, :]),
        axis=1,
    )
    pieces = [(green_prev, base)]
    for offset in range(1, SPAN + 1):
        pieces.append((passed_along(green_prev, "energy", -offset), base + offset))
        pieces.append((passed_along(green_prev, "energy", offset), base - offset))
    total = 0.0
    for piece, position in pieces:
        total = total + jnp.sum(chosen * (source[0] == position)) * piece[0, 0]
    return total


def on_device(
    energies, hamiltonian, coupling, green_prev, profile, phonon_weights, source, weight_index, left_face, right_face,
):
    width, faces = hamiltonian.shape[1], coupling.shape[1]
    slab_count = lax.axis_size("slab")
    first = (lax.axis_index("slab") == 0).astype(jnp.int32)[None]
    sig = exchange(green_prev, phonon_weights, source, weight_index)
    block = (width, width)
    face = (faces, 2 * faces)
    ham, coup = hamiltonian[0], coupling[0]
    (sent,) = call(first_kernel, [face], [energies], ham, profile, sig, coup, left_face, right_face)
    for turn in range(1, slab_count):
        incoming = passed_along(sent, "slab", 1)
        sent, message, e, q, a, scale = call(
            next_kernel,
            [face, face, (DOUBLINGS, *block), (DOUBLINGS, *block), (2, *block)],
            [energies, first],
            ham, profile, sig, coup, left_face, right_face, incoming,
            scalar_outs=[(1,)],
        )
    incoming = passed_along(message, "slab", -1)
    for turn in range(2, slab_count):
        (message,) = call(message_kernel, [face], [], sent, incoming, coup, left_face, right_face, ham)
        incoming = passed_along(message, "slab", -1)
    g, cols, rows = call(
        full_kernel, [(2, *block), (2 * width, faces), (faces, 2 * width)], [scale], e, q, a, right_face
    )
    (green,) = call(last_kernel, [(1, 1, 2, *block)], [], g, cols, rows, incoming)
    return green


def solution(mesh):
    in_specs = (
        P("energy"),
        P("slab", None, None),
        P("slab", None, None),
        P("energy", "slab", None, None, None),
        P(),
        P(),
        P("energy", None),
        P("energy", None),
        P("slab", None),
        P("slab", None),
    )
    out_specs = P("energy", "slab", None, None, None)
    return jax.shard_map(on_device, mesh=mesh, in_specs=in_specs, out_specs=out_specs, check_vma=False)
```

```python
import jax
import jax.numpy as jnp
from jax import lax
from jax.experimental import pallas as pl
from jax.experimental.pallas import tpu as pltpu
from jax.sharding import PartitionSpec as P

SPAN = 5
BROAD = 0.02
DOUBLINGS = 4

f32 = jnp.float32
bf16 = jnp.bfloat16
NN = (((1,), (0,)), ((), ()))
NT = (((1,), (1,)), ((), ()))
TN = (((0,), (0,)), ((), ()))


def split(x):
    high = x.astype(bf16)
    return high, (x - high.astype(f32)).astype(bf16)


def mm(a, b, dims=NN):
    return lax.dot_general(a, b, dims, preferred_element_type=f32)


def left3(*terms):
    out = []
    for x in terms:
        high, low = split(x)
        out += [high, high, low]
    return jnp.concatenate(out, axis=1)


def right3(*terms, axis=0):
    out = []
    for x in terms:
        high, low = split(x)
        out += [high, low, high]
    return jnp.concatenate(out, axis=axis)


def pair(x, axis):
    return jnp.concatenate(split(x), axis=axis)


def twice(x, axis):
    return jnp.concatenate([x, x], axis=axis)


def both(x_re, x_im):
    return jnp.concatenate([x_re, x_im], axis=0)


def skew(e):
    return 0.5 * (e - e.T)


def herm_left(e, q):
    return left3(e, -2.0 * q)


def any_left(y_re, y_im):
    return jnp.concatenate([left3(y_re, -(y_re + y_im)), left3(y_im, y_re - y_im)], axis=0)


def complex_mm(a_re, a_im, b_re, b_im):
    rows = a_re.shape[0]
    out = mm(
        jnp.concatenate([left3(a_re, -a_im), left3(a_im, a_re)], axis=0), right3(b_re, b_im)
    )
    return out[:rows], out[rows:]


def one_hot(width, face):
    return (lax.broadcasted_iota(jnp.int32, (width, face.shape[1]), 0) == face).astype(bf16)


def unit_of(width):
    row = lax.broadcasted_iota(jnp.int32, (width, width), 0)
    return (row == lax.broadcasted_iota(jnp.int32, (width, width), 1)).astype(f32)


def bounded(base_re, base_im, coup, left, in_re, in_im):
    width = base_re.shape[0]
    placed = mm(twice(one_hot(width, left), 1), pair(coup, 1), NT)
    t_re = mm(left3(placed), right3(in_re))
    t_im = mm(left3(placed), right3(in_im))
    bound = mm(both(left3(t_re), left3(t_im)), right3(placed, axis=1), NT)
    return base_re - bound[:width], base_im - bound[width:]


def begin(a_re, a_im):
    total = a_re + a_im
    gram = mm(left3(total, -2.0 * a_re), right3(total, a_im, axis=1), NT)
    modulus = jnp.sqrt(a_re * a_re + a_im * a_im)
    col_norm = jnp.max(jnp.sum(modulus, axis=0))
    row_norm = jnp.max(jnp.sum(modulus, axis=1))
    scale = 1.0 / (col_norm * row_norm)
    e = unit_of(a_re.shape[0]) - scale * gram
    return e, (-scale) * skew(gram), scale


def corner(a_re, a_im, right):
    width, faces = a_re.shape[0], right.shape[1]
    hot = one_hot(width, right)
    e, q, scale = begin(a_re, a_im)
    picked = twice(hot.T, 1)
    y_re = scale * mm(picked, pair(a_re, 1), NT)
    y_im = -scale * mm(picked, pair(a_im, 1), NT)
    powers = []
    for turn in range(DOUBLINGS):
        powers.append((e, q))
        weights = right3(e, q)
        if turn < DOUBLINGS - 1:
            out = mm(jnp.concatenate([herm_left(e, q), any_left(y_re, y_im)], axis=0), weights)
            e = out[:width]
            q = skew(e)
            out = out[width:]
        else:
            out = mm(any_left(y_re, y_im), weights)
        y_re = y_re + out[:faces]
        y_im = y_im + out[faces:]
    out = mm(any_left(y_re, y_im), weights)
    out = mm(any_left(out[:faces], out[faces:]), weights)
    y_re = y_re + out[:faces]
    y_im = y_im + out[faces:]
    face = mm(pair(both(y_re, y_im), 1), twice(hot, 0))
    return face[:faces], face[faces:], powers, scale


def lead_face(faces):
    return jnp.zeros((faces, faces), f32), -0.5 * unit_of(faces)


ROWS = 8


def over_x(e):
    return e ^ 2


def twin(e):
    return e ^ 1


def group_1(e):
    return e + 4 if e % 2 == 0 else e - 4


def group_2(e):
    return e - 4 if e % 2 == 0 else e + 4


def sent(value, pairs):
    return lax.ppermute(value, "energy", pairs)


def pairs_of(target, count):
    return [(e, target(e)) for e in range(count) if 0 <= target(e) < count]


def pack_kernel(source, weight_index, table, green, re_out, im_out):
    width = green.shape[3]
    re_out[:width] = green[0, 0, 0]
    im_out[:width] = green[0, 0, 1]
    row = lax.broadcasted_iota(jnp.int32, (ROWS, width), 0)
    rows = jnp.zeros((ROWS, width), f32)
    for term in range(2):
        rows = jnp.where(row == term, source[0, term].astype(f32), rows)
        rows = jnp.where(row == 2 + term, table[weight_index[0, term]], rows)
    re_out[width:] = rows
    im_out[width:] = rows


def coef_of(source, weight_index, table, index):
    weight = jnp.float32(0.0)
    for term in range(2):
        weight += jnp.where(source[0, term] == index, table[weight_index[0, term]], 0.0)
    return weight


def coef(rows, index):
    at = index.astype(f32)
    return jnp.where(rows[0:1] == at, rows[2:3], 0.0) + jnp.where(rows[1:2] == at, rows[3:4], 0.0)


def held(e):
    step = jnp.where(e % 2 == 0, 4, -4)
    other = e + 1 - 2 * (e % 2)
    return other, e - step, e + step, other + step, other - step


def outward_kernel(mine, pair, one, two, pair_one, pair_two, x, pair_x, near, over_x_out, out_1, out_2):
    width = mine.shape[3]
    e = lax.axis_index("energy")
    other, at_one, at_two, at_pair_one, at_pair_two = held(e)
    rows = x[width:]
    total = coef(rows, e) * mine[0, 0, 0] + coef(rows, other) * pair[0, 0, 0]
    total += coef(rows, at_one) * one[:width] + coef(rows, at_two) * two[:width]
    total += coef(rows, at_pair_one) * pair_one[:width] + coef(rows, at_pair_two) * pair_two[:width]
    over_x_out[...] = total
    across = e + 2 - 4 * ((e // 2) % 2)
    pair_across = other + 2 - 4 * ((other // 2) % 2)
    for target, rows, out in ((at_two, two[width:], out_1), (at_one, one[width:], out_2)):
        upward = target > e
        near_index = jnp.where(upward, e - 1, e + 1)
        counts = e % 4 == jnp.where(upward, 0, 3)
        total = coef(rows, e) * mine[0, 0, 1] + coef(rows, other) * pair[0, 0, 1]
        total += coef(rows, across) * x[:width] + coef(rows, pair_across) * pair_x[:width]
        out[...] = total + jnp.where(counts, coef(rows, near_index), 0.0) * near[:width]


def own_kernel(source, weight_index, table, mine, pair, one, two, pair_one, pair_two, x, pair_x, own_out):
    width = mine.shape[3]
    e = lax.axis_index("energy")
    other, at_one, at_two, at_pair_one, at_pair_two = held(e)
    across = e + 2 - 4 * ((e // 2) % 2)
    pair_across = other + 2 - 4 * ((other // 2) % 2)

    def weight(index):
        return coef_of(source, weight_index, table, index)

    total = weight(e) * mine[0, 0, 0] + weight(other) * pair[0, 0, 0]
    total += weight(at_one) * one[:width] + weight(at_two) * two[:width]
    own_out[0] = total + weight(at_pair_one) * pair_one[:width] + weight(at_pair_two) * pair_two[:width]
    total = weight(e) * mine[0, 0, 1] + weight(other) * pair[0, 0, 1]
    own_out[1] = total + weight(across) * x[:width] + weight(pair_across) * pair_x[:width]


def first_kernel(energy, source, weight_index, table, ham, profile, own, over_x, far, over_1, over_2, coup, left, right, face_out, base_out):
    width, faces = ham.shape[1], coup.shape[1]
    e = lax.axis_index("energy")
    far_index = jnp.where(e % 4 == 3, e + SPAN, e - SPAN)
    weight = coef_of(source, weight_index, table, far_index)
    sig_re = own[0] + over_x[...] + weight * far[:width]
    sig_im = own[1] + over_1[...] + over_2[...]
    unit = unit_of(width)
    base_re = energy[0] * unit - ham[0] - profile[...] * sig_re
    base_im = BROAD * unit - profile[...] * sig_im
    base_out[0] = base_re
    base_out[1] = base_im
    a_re, a_im = bounded(base_re, base_im, coup[0], left[...], *lead_face(faces))
    f_re, f_im, _, _ = corner(a_re, a_im, right[...])
    face_out[:, :faces] = f_re
    face_out[:, faces:] = f_im


def message_of(f_re, f_im, m_re, m_im, coup, left, right, width):
    faces = coup.shape[0]
    order = mm(one_hot(width, left), one_hot(width, right), TN).astype(bf16)
    mixed = mm(pair(coup, 1), twice(order, 0))
    if m_re is not None:
        t_re, t_im = complex_mm(f_re, f_im, m_re, m_im)
        c_re, c_im = complex_mm(t_re, t_im, f_re, f_im)
        f_re, f_im = f_re + c_re, f_im + c_im
    t = mm(left3(both(f_re, f_im)), right3(mixed, axis=1), NT)
    wide = jnp.concatenate([t[:faces], t[faces:]], axis=1)
    return mm(left3(mixed), right3(wide))


def next_kernel(
    base, coup, left, right, incoming,
    face_out, message_out, e_out, q_out, a_out, scale_out,
):
    width, faces = base.shape[1], coup.shape[1]
    lead_re, lead_im = lead_face(faces)
    is_first = lax.axis_index("slab") == 0
    in_re = jnp.where(is_first, lead_re, incoming[:, :faces])
    in_im = jnp.where(is_first, lead_im, incoming[:, faces:])
    a_re, a_im = bounded(base[0], base[1], coup[0], left[...], in_re, in_im)
    f_re, f_im, powers, scale = corner(a_re, a_im, right[...])
    face_out[:, :faces] = f_re
    face_out[:, faces:] = f_im
    message_out[...] = message_of(f_re, f_im, None, None, coup[0], left[...], right[...], width)
    for turn, (e, q) in enumerate(powers):
        e_out[turn] = e
        q_out[turn] = q
    a_out[0] = a_re
    a_out[1] = a_im
    scale_out[0] = scale


def message_kernel(face, message, coup, left, right, base, message_out):
    faces = coup.shape[1]
    message_out[...] = message_of(
        face[:, :faces], face[:, faces:], message[:, :faces], message[:, faces:],
        coup[0], left[...], right[...], base.shape[1],
    )


def full_kernel(scale, e_in, q_in, a_in, right, g_out, cols_out, rows_out):
    width, faces = a_in.shape[1], right.shape[1]
    unit = unit_of(width)
    s_e, s_q = unit + e_in[0], q_in[0]
    for turn in range(1, DOUBLINGS):
        e, q = e_in[turn], q_in[turn]
        weights = right3(e, q)
        if turn < DOUBLINGS - 1:
            s_e = s_e + mm(herm_left(s_e, s_q), weights)
        else:
            out = mm(jnp.concatenate([herm_left(s_e, s_q), herm_left(e, q)], axis=0), weights)
            s_e = s_e + out[:width]
            e = out[width:]
        s_q = skew(s_e)
    s_e = s_e + mm(herm_left(s_e, s_q), right3(e, skew(e)))
    s_q = skew(s_e)
    b, c = a_in[0].T, a_in[1].T
    g = scale[0] * mm(any_left(b, -c), right3(s_e, s_q))
    g_out[0] = g[:width]
    g_out[1] = g[width:]
    hot = one_hot(width, right[...])
    high, low = split(g)
    cols_out[...] = mm(jnp.concatenate([high, low], axis=1), twice(hot, 0))
    wide_high = jnp.concatenate([high[:width], high[width:]], axis=1)
    wide_low = jnp.concatenate([low[:width], low[width:]], axis=1)
    rows_out[...] = mm(twice(hot.T, 1), jnp.concatenate([wide_high, wide_low], axis=0))


def last_kernel(g, cols, rows, message, green_out):
    width, faces = g.shape[1], message.shape[0]
    t_re, t_im = complex_mm(
        message[:, :faces], message[:, faces:], rows[:, :width], rows[:, width:]
    )
    c_re, c_im = complex_mm(cols[:width], cols[width:], t_re, t_im)
    green_out[0, 0, 0] = g[0] + c_re
    green_out[0, 0, 1] = g[1] + c_im


def call(kernel, outs, scalars, *arrays, scalar_outs=()):
    smem = pl.BlockSpec(memory_space=pltpu.SMEM)
    vmem = pl.BlockSpec(memory_space=pltpu.VMEM)
    return pl.pallas_call(
        kernel,
        out_shape=[jax.ShapeDtypeStruct(shape, f32) for shape in (*outs, *scalar_outs)],
        in_specs=[smem] * len(scalars) + [vmem] * len(arrays),
        out_specs=[vmem] * len(outs) + [smem] * len(scalar_outs),
        compiler_params=pltpu.CompilerParams(vmem_limit_bytes=40 * 2**20),
    )(*scalars, *arrays)


def exchange(green_prev, phonon_weights, source, weight_index):
    count = lax.axis_size("energy")
    width = green_prev.shape[-1]
    scalars = [source, weight_index, phonon_weights]
    block, tagged = (width, width), (width + ROWS, width)
    all_twin, all_x = pairs_of(twin, count), pairs_of(over_x, count)
    all_1, all_2 = pairs_of(group_1, count), pairs_of(group_2, count)
    groups = count // 4
    near_pairs = [(4 * k, 4 * k - 1) for k in range(2, groups)] + [(4 * k + 3, 4 * k + 4) for k in range(groups - 2)]
    far_pairs = [p for k in range(1, groups - 1) for p in ((4 * k, 4 * k - 1), (4 * k + 3, 4 * k + 4))]
    pair = sent(green_prev, all_twin)
    re, im = call(pack_kernel, [tagged, tagged], scalars, green_prev)
    x = sent(im, all_x)
    one = sent(re, all_1)
    two = sent(re, all_2)
    near = sent(im, near_pairs)
    pair_x = sent(x, all_twin)
    pair_one = sent(one, all_twin)
    pair_two = sent(two, all_twin)
    far = sent(two, far_pairs)
    over_x_sum, sum_1, sum_2 = call(
        outward_kernel, [block] * 3, [], green_prev, pair, one, two, pair_one, pair_two, x, pair_x, near
    )
    from_x = sent(over_x_sum, all_x)
    from_1 = sent(sum_1, all_1)
    from_2 = sent(sum_2, all_2)
    (own,) = call(own_kernel, [(2, *block)], scalars, green_prev, pair, one, two, pair_one, pair_two, x, pair_x)
    return own, from_x, far, from_1, from_2


def passed_along(value, steps):
    count = lax.axis_size("slab")
    initial, last = (max(0, -steps), min(count, count - steps))
    return lax.ppermute(value, "slab", [(start, start + steps) for start in range(initial, last)])


def on_device(
    energies, hamiltonian, coupling, green_prev, profile, phonon_weights, source, weight_index, left_face, right_face,
):
    width, faces = hamiltonian.shape[1], coupling.shape[1]
    slab_count = lax.axis_size("slab")
    block, face = (width, width), (faces, 2 * faces)
    own, from_x, far, from_1, from_2 = exchange(green_prev, phonon_weights, source, weight_index)
    face_sent, base = call(
        first_kernel, [face, (2, *block)], [energies, source, weight_index, phonon_weights],
        hamiltonian, profile, own, from_x, far, from_1, from_2, coupling, left_face, right_face,
    )
    for turn in range(1, slab_count):
        incoming = passed_along(face_sent, 1)
        face_sent, message, e, q, a, scale = call(
            next_kernel,
            [face, face, (DOUBLINGS, *block), (DOUBLINGS, *block), (2, *block)],
            [], base, coupling, left_face, right_face, incoming,
            scalar_outs=[(1,)],
        )
    incoming = passed_along(message, -1)
    for turn in range(2, slab_count):
        (message,) = call(message_kernel, [face], [], face_sent, incoming, coupling, left_face, right_face, base)
        incoming = passed_along(message, -1)
    g, cols, rows = call(
        full_kernel, [(2, *block), (2 * width, faces), (faces, 2 * width)], [scale], e, q, a, right_face
    )
    (green,) = call(last_kernel, [(1, 1, 2, *block)], [], g, cols, rows, incoming)
    return green


def solution(mesh):
    in_specs = (
        P("energy"),
        P("slab", None, None),
        P("slab", None, None),
        P("energy", "slab", None, None, None),
        P(),
        P(),
        P("energy", None),
        P("energy", None),
        P("slab", None),
        P("slab", None),
    )
    out_specs = P("energy", "slab", None, None, None)
    return jax.shard_map(on_device, mesh=mesh, in_specs=in_specs, out_specs=out_specs, check_vma=False)
```

```python
import functools

import jax
import jax.numpy as jnp
from jax import lax
from jax.experimental import pallas as pl
from jax.experimental.pallas import tpu as pltpu
from jax.sharding import PartitionSpec as P

SPAN = 5
BROAD = 0.02
DOUBLINGS = 4

f32 = jnp.float32
bf16 = jnp.bfloat16
NN = (((1,), (0,)), ((), ()))
NT = (((1,), (1,)), ((), ()))
TN = (((0,), (0,)), ((), ()))


def split(x):
    high = x.astype(bf16)
    return high, (x - high.astype(f32)).astype(bf16)


def mm(a, b, dims=NN):
    return lax.dot_general(a, b, dims, preferred_element_type=f32)


def left3(*terms):
    out = []
    for x in terms:
        high, low = split(x)
        out += [high, high, low]
    return jnp.concatenate(out, axis=1)


def right3(*terms, axis=0):
    out = []
    for x in terms:
        high, low = split(x)
        out += [high, low, high]
    return jnp.concatenate(out, axis=axis)


def pair(x, axis):
    return jnp.concatenate(split(x), axis=axis)


def twice(x, axis):
    return jnp.concatenate([x, x], axis=axis)


def both(x_re, x_im):
    return jnp.concatenate([x_re, x_im], axis=0)


def skew(e):
    return 0.5 * (e - e.T)


def stack(*parts):
    return jnp.concatenate(parts, axis=0)


def left_of(high, low):
    return jnp.concatenate([high, high, low], axis=1)


def right_of(high, low):
    return jnp.concatenate([high, low, high], axis=0)


def herm(e, q):
    return split(e), split(q)


def times(s, h):
    return mm(left_of(*s[0]), right_of(*h[0])) - 2.0 * mm(left_of(*s[1]), right_of(*h[1]))


def rows_times(e_rows, q_rows, h):
    count = e_rows.shape[0]
    e_high, e_low = split(e_rows)
    q_high, q_low = split(q_rows)
    from_e = mm(stack(e_high, e_low), h[0][0])
    from_q = mm(stack(q_high, q_low), h[1][0])
    lows = mm(e_high, h[0][1]) + mm(q_high, h[1][1])
    return (from_e[:count] + from_e[count:]) + (from_q[:count] + from_q[count:]) + lows


def thin_times(y_re, y_im, h):
    out = rows_times(stack(y_re, y_im), stack(-(y_re + y_im), y_re - y_im), h)
    return out[:y_re.shape[0]], out[y_re.shape[0]:]


def complex_mm(a_re, a_im, b_re, b_im):
    rows = a_re.shape[0]
    out = mm(stack(left3(a_re, -a_im), left3(a_im, a_re)), right3(b_re, b_im))
    return out[:rows], out[rows:]


def one_hot(width, face):
    return (lax.broadcasted_iota(jnp.int32, (width, face.shape[1]), 0) == face).astype(bf16)


def unit_of(width):
    row = lax.broadcasted_iota(jnp.int32, (width, width), 0)
    return (row == lax.broadcasted_iota(jnp.int32, (width, width), 1)).astype(f32)


def begin(a_re, a_im):
    total = a_re + a_im
    gram = mm(left3(total), right3(total, axis=1), NT) - mm(left3(2.0 * a_re), right3(a_im, axis=1), NT)
    modulus = jnp.sqrt(a_re * a_re + a_im * a_im)
    col_norm = jnp.max(jnp.sum(modulus, axis=0))
    row_norm = jnp.max(jnp.sum(modulus, axis=1))
    scale = 1.0 / (col_norm * row_norm)
    return unit_of(a_re.shape[0]) - scale * gram, (-scale) * skew(gram), scale


def corner(a_re, a_im, proj, series=False):
    width, faces = proj.shape
    e, q, scale = begin(a_re, a_im)
    proj_t = proj.T
    y = scale * mm(left3(proj_t), right3(both(a_re, a_im), axis=1), NT)
    y_re, y_im = y[:, :width], -y[:, width:]
    s_e, s_q = unit_of(width) + e, q
    for turn in range(1, DOUBLINGS):
        h = herm(e, q)
        if series and turn > 1:
            s_e = s_e + times(herm(s_e, s_q), h)
            s_q = skew(s_e)
        e = times(h, h)
        q = skew(e)
        c_re, c_im = thin_times(y_re, y_im, h)
        y_re, y_im = y_re + c_re, y_im + c_im
    h = herm(e, q)
    c_re, c_im = thin_times(y_re, y_im, h)
    y_re, y_im = y_re + c_re, y_im + c_im
    none = jnp.zeros_like(proj_t)
    t_re, t_im = thin_times(proj_t, none, h)
    u_re, u_im = thin_times(y_re, y_im, h)
    out = mm(left3(both(y_re, y_im)), right3(proj))
    out += mm(stack(left3(u_re, u_im), left3(u_im, -u_re)), right3(t_re, t_im, axis=1), NT)
    return out[:faces], out[faces:], (s_e, s_q, e, q), scale


def series_of(e, q):
    s_e, s_q = unit_of(e.shape[0]) + e, q
    for turn in range(1, DOUBLINGS):
        h = herm(e, q)
        if turn > 1:
            s_e = s_e + times(herm(s_e, s_q), h)
            s_q = skew(s_e)
        e = times(h, h)
        q = skew(e)
    return s_e, s_q, e, q


def full(a_re, a_im, s_e, s_q, e, q, scale):
    h = herm(e, q)
    s_e = s_e + times(herm(s_e, s_q), h)
    e = times(h, h)
    s_e = s_e + times(herm(s_e, skew(s_e)), herm(e, skew(e)))
    s_q = skew(s_e)
    s_p = s_e - s_q
    b, c = a_re.T, a_im.T
    one = mm(left3(b - c), right3(s_p))
    g_re = one + mm(left3(c), right3(s_e))
    g_im = one + mm(left3(b), right3(s_q - s_p))
    return scale * g_re, scale * g_im


ROWS = 8


def over_x(e):
    return e ^ 2


def twin(e):
    return e ^ 1


def group_1(e):
    return e + 4 if e % 2 == 0 else e - 4


def group_2(e):
    return e - 4 if e % 2 == 0 else e + 4


def sent(value, pairs):
    return lax.ppermute(value, "energy", pairs)


def pairs_of(target, count):
    return [(e, target(e)) for e in range(count) if 0 <= target(e) < count]


def pack_kernel(energy_hbm, source_hbm, index_hbm, table_hbm, green, im_out, re_out, energy, source, index, table, sems):
    width = green.shape[3]
    copies = [
        pltpu.make_async_copy(start, end, sems.at[k])
        for k, (start, end) in enumerate((
            (energy_hbm, energy), (source_hbm, source), (index_hbm, index), (table_hbm, table),
            (green.at[0, 0, 1], im_out.at[pl.ds(0, width)]), (green.at[0, 0, 0], re_out.at[pl.ds(0, width)]),
        ))
    ]
    for copy in copies:
        copy.start()
    for copy in copies[:4]:
        copy.wait()
    row = lax.broadcasted_iota(jnp.int32, (ROWS, width), 0)
    rows = jnp.where(row == 4, energy[0], 0.0)
    for term in range(2):
        rows = jnp.where(row == term, source[0, term].astype(f32), rows)
        rows = jnp.where(row == 2 + term, table[index[0, term]], rows)
    im_out[width:] = rows
    re_out[width:] = rows
    for copy in copies[4:]:
        copy.wait()


def pack(green_prev, energies, source, weight_index, table):
    width = green_prev.shape[-1]
    hbm, vmem = pl.BlockSpec(memory_space=pltpu.HBM), pl.BlockSpec(memory_space=pltpu.VMEM)
    return pl.pallas_call(
        pack_kernel,
        out_shape=[jax.ShapeDtypeStruct((width + ROWS, width), f32)] * 2,
        in_specs=[hbm] * 5,
        out_specs=[vmem] * 2,
        scratch_shapes=[
            pltpu.SMEM(energies.shape, f32), pltpu.SMEM(source.shape, jnp.int32),
            pltpu.SMEM(weight_index.shape, jnp.int32), pltpu.SMEM(table.shape, f32),
            pltpu.SemaphoreType.DMA((6,)),
        ],
        compiler_params=pltpu.CompilerParams(vmem_limit_bytes=40 * 2**20),
    )(energies, source, weight_index, table, green_prev)


def coef(rows, index):
    at = index.astype(f32)
    return jnp.where(rows[0:1] == at, rows[2:3], 0.0) + jnp.where(rows[1:2] == at, rows[3:4], 0.0)


def held(e):
    step = jnp.where(e % 2 == 0, 4, -4)
    other = e + 1 - 2 * (e % 2)
    return other, e - step, e + step, other + step, other - step


def over_x_kernel(re, twin_block, one, two, pair_one, pair_two, x, out):
    width = re.shape[1]
    e = lax.axis_index("energy")
    other, at_one, at_two, at_pair_one, at_pair_two = held(e)
    rows = x[width:]
    total = coef(rows, e) * re[:width] + coef(rows, other) * twin_block[0, 0, 0]
    total += coef(rows, at_one) * one[:width] + coef(rows, at_two) * two[:width]
    out[...] = total + coef(rows, at_pair_one) * pair_one[:width] + coef(rows, at_pair_two) * pair_two[:width]


def groups_kernel(im, twin_block, x, pair_x, near, one, two, out_1, out_2):
    width = im.shape[1]
    e = lax.axis_index("energy")
    other, at_one, at_two, _, _ = held(e)
    across = e + 2 - 4 * ((e // 2) % 2)
    pair_across = other + 2 - 4 * ((other // 2) % 2)
    for target, rows, out in ((at_two, two[width:], out_1), (at_one, one[width:], out_2)):
        upward = target > e
        near_index = jnp.where(upward, e - 1, e + 1)
        counts = e % 4 == jnp.where(upward, 0, 3)
        total = coef(rows, e) * im[:width] + coef(rows, other) * twin_block[0, 0, 1]
        total += coef(rows, across) * x[:width] + coef(rows, pair_across) * pair_x[:width]
        out[...] = total + jnp.where(counts, coef(rows, near_index), 0.0) * near[:width]


def own_kernel(re, im, twin_block, one, two, pair_one, pair_two, x, pair_x, ham, profile, coup, left, base_out, placed_out):
    width = re.shape[1]
    e = lax.axis_index("energy")
    other, at_one, at_two, at_pair_one, at_pair_two = held(e)
    across = e + 2 - 4 * ((e // 2) % 2)
    pair_across = other + 2 - 4 * ((other // 2) % 2)
    rows = re[width:]
    total = coef(rows, e) * re[:width] + coef(rows, other) * twin_block[0, 0, 0]
    total += coef(rows, at_one) * one[:width] + coef(rows, at_two) * two[:width]
    total += coef(rows, at_pair_one) * pair_one[:width] + coef(rows, at_pair_two) * pair_two[:width]
    unit = unit_of(width)
    base_out[0] = rows[4:5] * unit - ham[0] - profile[...] * total
    total = coef(rows, e) * im[:width] + coef(rows, other) * twin_block[0, 0, 1]
    total += coef(rows, across) * x[:width] + coef(rows, pair_across) * pair_x[:width]
    placed = mm(twice(one_hot(width, left[...]), 1), pair(coup[0], 1), NT)
    placed_out[...] = placed
    lead = jnp.where(lax.axis_index("slab") == 0, -0.5, 0.0) * mm(left3(placed), right3(placed, axis=1), NT)
    base_out[1] = BROAD * unit - profile[...] * total - lead


def first_kernel(own, re, profile, from_x, far, from_1, from_2, right, face_out, base_out):
    width, faces = profile.shape[0], right.shape[1]
    e = lax.axis_index("energy")
    weight = coef(re[width:], jnp.where(e % 4 == 3, e + SPAN, e - SPAN))
    base_re = own[0] - profile[...] * (from_x[...] + weight * far[:width])
    base_im = own[1] - profile[...] * (from_1[...] + from_2[...])
    base_out[0] = base_re
    base_out[1] = base_im

    @pl.when(lax.axis_index("slab") == 0)
    def _():
        f_re, f_im, _, _ = corner(base_re, base_im, one_hot(width, right[...]).astype(f32))
        face_out[:, :faces] = f_re
        face_out[:, faces:] = f_im


def bounded(base, placed, incoming):
    width, faces = placed.shape
    is_first = lax.axis_index("slab") == 0
    face = jnp.where(is_first, 0.0, incoming[...])
    split_placed = left3(placed[...])
    t = mm(split_placed, right3(face))
    bound = mm(stack(left3(t[:, :faces]), left3(t[:, faces:])), right3(placed[...], axis=1), NT)
    return base[0] - bound[:width], base[1] - bound[width:]


def face_kernel(base, placed, incoming, right, face_out):
    width, faces = placed.shape
    a_re, a_im = bounded(base, placed, incoming)
    f_re, f_im, _, _ = corner(a_re, a_im, one_hot(width, right[...]).astype(f32))
    face_out[:, :faces] = f_re
    face_out[:, faces:] = f_im


def face_parts(g_re, g_im, right, cols_out, rows_out):
    width = g_re.shape[0]
    hot = one_hot(width, right[...])
    high, low = split(both(g_re, g_im))
    cols_out[...] = mm(jnp.concatenate([high, low], axis=1), twice(hot, 0))
    wide_high = jnp.concatenate([high[:width], high[width:]], axis=1)
    wide_low = jnp.concatenate([low[:width], low[width:]], axis=1)
    rows_out[...] = mm(twice(hot.T, 1), stack(wide_high, wide_low))


def whole(a_re, a_im, right, g_out, cols_out, rows_out):
    e, q, scale = begin(a_re, a_im)
    g_re, g_im = full(a_re, a_im, *series_of(e, q), scale)
    g_out[0] = g_re
    g_out[1] = g_im
    face_parts(g_re, g_im, right, cols_out, rows_out)


def slab_0_kernel(base, right, g_out, cols_out, rows_out):
    @pl.when(lax.axis_index("slab") == 0)
    def _():
        whole(base[0], base[1], right, g_out, cols_out, rows_out)


def middle_kernel(slabs, base, placed, incoming, right, g, cols, rows, g_out, cols_out, rows_out):
    slab = lax.axis_index("slab")

    @pl.when((slab != 0) & (slab != slabs - 1))
    def _():
        a_re, a_im = bounded(base, placed, incoming)
        whole(a_re, a_im, right, g_out, cols_out, rows_out)

    @pl.when((slab == 0) | (slab == slabs - 1))
    def _():
        g_out[...] = g[...]
        cols_out[...] = cols[...]
        rows_out[...] = rows[...]


def turn_kernel(slabs, base, placed, incoming, message_out, series_out, a_out, scale_out):
    @pl.when(lax.axis_index("slab") == slabs - 1)
    def _():
        width, faces = placed.shape
        a_re, a_im = bounded(base, placed, incoming)
        m_re, m_im, series, scale = corner(a_re, a_im, placed[...], series=True)
        message_out[:, :faces] = m_re
        message_out[:, faces:] = m_im
        for k, part in enumerate(series):
            series_out[k] = part
        a_out[0] = a_re
        a_out[1] = a_im
        scale_out[0] = scale


def message_kernel(slabs, cols, rows, message, coup, left, right, base, message_out):
    width, faces = base.shape[1], coup.shape[1]
    hot = one_hot(width, right[...])
    f = mm(twice(hot.T, 1), pair(cols[...].reshape(2 * width, faces)[:width], 0))
    f_im = mm(twice(hot.T, 1), pair(cols[width:], 0))
    order = mm(one_hot(width, left[...]), hot, TN).astype(bf16)
    mixed = mm(pair(coup[0], 1), twice(order, 0))
    t_re, t_im = complex_mm(f, f_im, message[:, :faces], message[:, faces:])
    c_re, c_im = complex_mm(t_re, t_im, f, f_im)
    t = mm(left3(both(f + c_re, f_im + c_im)), right3(mixed, axis=1), NT)
    wide = jnp.concatenate([t[:faces], t[faces:]], axis=1)
    is_last = lax.axis_index("slab") == slabs - 1

    @pl.when(jnp.logical_not(is_last))
    def _():
        message_out[...] = mm(left3(mixed), right3(wide))

    @pl.when(is_last)
    def _():
        message_out[...] = message[...]


def last_full_kernel(slabs, scale, series, a_in, green_out, block, sems):
    @pl.when(lax.axis_index("slab") == slabs - 1)
    def _():
        block[0], block[1] = full(a_in[0], a_in[1], *(series[k] for k in range(4)), scale[0])
        copies = [pltpu.make_async_copy(block.at[k], green_out.at[0, 0, k], sems.at[k]) for k in range(2)]
        for copy in copies:
            copy.start()
        for copy in copies:
            copy.wait()


def last_kernel(slabs, g, cols, rows, message, given, green_out, block, sems):
    @pl.when(lax.axis_index("slab") != slabs - 1)
    def _():
        width, faces = g.shape[1], message.shape[0]
        t_re, t_im = complex_mm(message[:, :faces], message[:, faces:], rows[:, :width], rows[:, width:])
        c_re, c_im = complex_mm(cols[:width], cols[width:], t_re, t_im)
        copies = []
        for k, change in enumerate((c_re, c_im)):
            block[k] = g[k] + change
            copies.append(pltpu.make_async_copy(block.at[k], green_out.at[0, 0, k], sems.at[k]))
            copies[k].start()
        for copy in copies:
            copy.wait()


def write_green(kernel, scalars, arrays, shape, given=None):
    smem, vmem, hbm = (pl.BlockSpec(memory_space=space) for space in (pltpu.SMEM, pltpu.VMEM, pltpu.HBM))
    more = [] if given is None else [given]
    inputs = len(scalars) + len(arrays)
    return pl.pallas_call(
        kernel,
        out_shape=jax.ShapeDtypeStruct(shape, f32),
        in_specs=[smem] * len(scalars) + [vmem] * len(arrays) + [hbm] * len(more),
        out_specs=hbm,
        scratch_shapes=[pltpu.VMEM(shape[2:], f32), pltpu.SemaphoreType.DMA((2,))],
        input_output_aliases={inputs: 0} if more else {},
        compiler_params=pltpu.CompilerParams(vmem_limit_bytes=40 * 2**20),
    )(*scalars, *arrays, *more)


def call(kernel, outs, scalars, *arrays, scalar_outs=()):
    smem = pl.BlockSpec(memory_space=pltpu.SMEM)
    vmem = pl.BlockSpec(memory_space=pltpu.VMEM)
    return pl.pallas_call(
        kernel,
        out_shape=[jax.ShapeDtypeStruct(shape, f32) for shape in (*outs, *scalar_outs)],
        in_specs=[smem] * len(scalars) + [vmem] * len(arrays),
        out_specs=[vmem] * len(outs) + [smem] * len(scalar_outs),
        compiler_params=pltpu.CompilerParams(vmem_limit_bytes=40 * 2**20),
    )(*scalars, *arrays)


def exchange(energies, hamiltonian, coupling, green_prev, profile, phonon_weights, source, weight_index, left_face):
    count = lax.axis_size("energy")
    width = green_prev.shape[-1]
    block = (width, width)
    all_twin, all_x = pairs_of(twin, count), pairs_of(over_x, count)
    all_1, all_2 = pairs_of(group_1, count), pairs_of(group_2, count)
    groups = count // 4
    near_pairs = [(4 * k, 4 * k - 1) for k in range(2, groups)] + [(4 * k + 3, 4 * k + 4) for k in range(groups - 2)]
    far_pairs = [p for k in range(1, groups - 1) for p in ((4 * k, 4 * k - 1), (4 * k + 3, 4 * k + 4))]
    pair = sent(green_prev, all_twin)
    im, re = pack(green_prev, energies, source, weight_index, phonon_weights)
    x = sent(im, all_x)
    one = sent(re, all_1)
    two = sent(re, all_2)
    near = sent(im, near_pairs)
    pair_one = sent(one, all_twin)
    pair_two = sent(two, all_twin)
    far = sent(two, far_pairs)
    pair_x = sent(x, all_twin)
    (over_x_sum,) = call(over_x_kernel, [block], [], re, pair, one, two, pair_one, pair_two, x)
    from_x = sent(over_x_sum, all_x)
    sum_1, sum_2 = call(
        groups_kernel, [block] * 2, [], im, pair, x, pair_x, near, one, two
    )
    from_1 = sent(sum_1, all_1)
    from_2 = sent(sum_2, all_2)
    own, placed = call(
        own_kernel, [(2, *block), (width, coupling.shape[1])], [],
        re, im, pair, one, two, pair_one, pair_two, x, pair_x, hamiltonian, profile, coupling, left_face,
    )
    return placed, (own, re, profile, from_x, far, from_1, from_2)


def passed_along(value, steps):
    count = lax.axis_size("slab")
    return lax.ppermute(value, "slab", [(start, (start + steps) % count) for start in range(count)])


def on_device(
    energies, hamiltonian, coupling, green_prev, profile, phonon_weights, source, weight_index, left_face, right_face,
):
    width, faces = hamiltonian.shape[1], coupling.shape[1]
    slabs = lax.axis_size("slab")
    block, face = (width, width), (faces, 2 * faces)
    parts_of_g = [(2, *block), (2 * width, faces), (faces, 2 * width)]
    placed, parts = exchange(
        energies, hamiltonian, coupling, green_prev, profile, phonon_weights, source, weight_index, left_face
    )
    face_sent, base = call(first_kernel, [face, (2, *block)], [], *parts, right_face)
    incoming = passed_along(face_sent, 1)
    for turn in range(1, slabs - 1):
        (face_sent,) = call(face_kernel, [face], [], base, placed, incoming, right_face)
        incoming = passed_along(face_sent, 1)
    g, cols, rows = call(slab_0_kernel, parts_of_g, [], base, right_face)
    placed, g = lax.optimization_barrier((placed, g))
    if slabs > 2:
        g, cols, rows = call(
            functools.partial(middle_kernel, slabs), parts_of_g, [], base, placed, incoming, right_face, g, cols, rows
        )
    message, series, a, scale = call(
        functools.partial(turn_kernel, slabs), [face, (4, *block), (2, *block)], [], base, placed, incoming,
        scalar_outs=[(1,)],
    )
    incoming = passed_along(message, -1)
    green = write_green(functools.partial(last_full_kernel, slabs), [scale], [series, a], green_prev.shape)
    for turn in range(2, slabs):
        (message,) = call(
            functools.partial(message_kernel, slabs), [face], [],
            cols, rows, incoming, coupling, left_face, right_face, base,
        )
        incoming = passed_along(message, -1)
    return write_green(functools.partial(last_kernel, slabs), [], [g, cols, rows, incoming], green_prev.shape, green)


def solution(mesh):
    in_specs = (
        P("energy"),
        P("slab", None, None),
        P("slab", None, None),
        P("energy", "slab", None, None, None),
        P(),
        P(),
        P("energy", None),
        P("energy", None),
        P("slab", None),
        P("slab", None),
    )
    out_specs = P("energy", "slab", None, None, None)
    return jax.shard_map(on_device, mesh=mesh, in_specs=in_specs, out_specs=out_specs, check_vma=False)
```

```python
import functools

import jax
import jax.numpy as jnp
from jax import lax
from jax.experimental import pallas as pl
from jax.experimental.pallas import tpu as pltpu
from jax.sharding import PartitionSpec as P

SPAN = 5
BROAD = 0.02
DOUBLINGS = 4

f32 = jnp.float32
bf16 = jnp.bfloat16
NN = (((1,), (0,)), ((), ()))
NT = (((1,), (1,)), ((), ()))
TN = (((0,), (0,)), ((), ()))


def split(x):
    high = x.astype(bf16)
    return high, (x - high.astype(f32)).astype(bf16)


def mm(a, b, dims=NN):
    return lax.dot_general(a, b, dims, preferred_element_type=f32)


def left3(*terms):
    out = []
    for x in terms:
        high, low = split(x)
        out += [high, high, low]
    return jnp.concatenate(out, axis=1)


def right3(*terms, axis=0):
    out = []
    for x in terms:
        high, low = split(x)
        out += [high, low, high]
    return jnp.concatenate(out, axis=axis)


def pair(x, axis):
    return jnp.concatenate(split(x), axis=axis)


def twice(x, axis):
    return jnp.concatenate([x, x], axis=axis)


def both(x_re, x_im):
    return jnp.concatenate([x_re, x_im], axis=0)


def skew(e):
    return 0.5 * (e - e.T)


def stack(*parts):
    return jnp.concatenate(parts, axis=0)


def left_of(high, low):
    return jnp.concatenate([high, high, low], axis=1)


def right_of(high, low):
    return jnp.concatenate([high, low, high], axis=0)


def herm(e, q):
    return split(e), split(q)


def times(s, h):
    return mm(left_of(*s[0]), right_of(*h[0])) - 2.0 * mm(left_of(*s[1]), right_of(*h[1]))


def rows_times(e_rows, q_rows, h):
    count = e_rows.shape[0]
    e_high, e_low = split(e_rows)
    q_high, q_low = split(q_rows)
    from_e = mm(stack(e_high, e_low), h[0][0])
    from_q = mm(stack(q_high, q_low), h[1][0])
    lows = mm(e_high, h[0][1]) + mm(q_high, h[1][1])
    return (from_e[:count] + from_e[count:]) + (from_q[:count] + from_q[count:]) + lows


def thin_times(y_re, y_im, h):
    out = rows_times(stack(y_re, y_im), stack(-(y_re + y_im), y_re - y_im), h)
    return out[:y_re.shape[0]], out[y_re.shape[0]:]


def complex_mm(a_re, a_im, b_re, b_im):
    rows = a_re.shape[0]
    out = mm(stack(left3(a_re, -a_im), left3(a_im, a_re)), right3(b_re, b_im))
    return out[:rows], out[rows:]


def one_hot(width, face):
    return (lax.broadcasted_iota(jnp.int32, (width, face.shape[1]), 0) == face).astype(bf16)


def unit_of(width):
    row = lax.broadcasted_iota(jnp.int32, (width, width), 0)
    return (row == lax.broadcasted_iota(jnp.int32, (width, width), 1)).astype(f32)


def begin(a_re, a_im):
    total = a_re + a_im
    gram = mm(left3(total), right3(total, axis=1), NT) - mm(left3(2.0 * a_re), right3(a_im, axis=1), NT)
    modulus = jnp.sqrt(a_re * a_re + a_im * a_im)
    col_norm = jnp.max(jnp.sum(modulus, axis=0))
    row_norm = jnp.max(jnp.sum(modulus, axis=1))
    scale = 1.0 / (col_norm * row_norm)
    return unit_of(a_re.shape[0]) - scale * gram, (-scale) * skew(gram), scale


def corner(a_re, a_im, proj):
    width, faces = proj.shape
    e, q, scale = begin(a_re, a_im)
    proj_t = proj.T
    y = scale * mm(left3(proj_t), right3(both(a_re, a_im), axis=1), NT)
    y_re, y_im = y[:, :width], -y[:, width:]
    powers = [e]
    for turn in range(1, DOUBLINGS):
        h = herm(e, q)
        e = times(h, h)
        q = skew(e)
        powers.append(e)
        c_re, c_im = thin_times(y_re, y_im, h)
        y_re, y_im = y_re + c_re, y_im + c_im
    h = herm(e, q)
    c_re, c_im = thin_times(y_re, y_im, h)
    y_re, y_im = y_re + c_re, y_im + c_im
    none = jnp.zeros_like(proj_t)
    t_re, t_im = thin_times(proj_t, none, h)
    u_re, u_im = thin_times(y_re, y_im, h)
    out = mm(left3(both(y_re, y_im)), right3(proj))
    out += mm(stack(left3(u_re, u_im), left3(u_im, -u_re)), right3(t_re, t_im, axis=1), NT)
    return out[:faces], out[faces:], powers, scale


def series_of(e, q):
    s_e, s_q = unit_of(e.shape[0]) + e, q
    for turn in range(1, DOUBLINGS):
        h = herm(e, q)
        if turn > 1:
            s_e = s_e + times(herm(s_e, s_q), h)
            s_q = skew(s_e)
        e = times(h, h)
        q = skew(e)
    return s_e, s_q, e, q


def full(a_re, a_im, s_e, s_q, e, q, scale):
    h = herm(e, q)
    s_e = s_e + times(herm(s_e, s_q), h)
    e = times(h, h)
    s_e = s_e + times(herm(s_e, skew(s_e)), herm(e, skew(e)))
    s_q = skew(s_e)
    s_p = s_e - s_q
    b, c = a_re.T, a_im.T
    one = mm(left3(b - c), right3(s_p))
    g_re = one + mm(left3(c), right3(s_e))
    g_im = one + mm(left3(b), right3(s_q - s_p))
    return scale * g_re, scale * g_im


ROWS = 8


def over_x(e):
    return e ^ 2


def twin(e):
    return e ^ 1


def group_1(e):
    return e + 4 if e % 2 == 0 else e - 4


def group_2(e):
    return e - 4 if e % 2 == 0 else e + 4


def sent(value, pairs):
    return lax.ppermute(value, "energy", pairs)


def pairs_of(target, count):
    return [(e, target(e)) for e in range(count) if 0 <= target(e) < count]


def pack_kernel(energy_hbm, source_hbm, index_hbm, table_hbm, green, im_out, re_out, energy, source, index, table, sems):
    width = green.shape[3]
    copies = [
        pltpu.make_async_copy(start, end, sems.at[k])
        for k, (start, end) in enumerate((
            (energy_hbm, energy), (source_hbm, source), (index_hbm, index), (table_hbm, table),
            (green.at[0, 0, 1], im_out.at[pl.ds(0, width)]), (green.at[0, 0, 0], re_out.at[pl.ds(0, width)]),
        ))
    ]
    for copy in copies:
        copy.start()
    for copy in copies[:4]:
        copy.wait()
    row = lax.broadcasted_iota(jnp.int32, (ROWS, width), 0)
    rows = jnp.where(row == 4, energy[0], 0.0)
    for term in range(2):
        rows = jnp.where(row == term, source[0, term].astype(f32), rows)
        rows = jnp.where(row == 2 + term, table[index[0, term]], rows)
    im_out[width:] = rows
    re_out[width:] = rows
    for copy in copies[4:]:
        copy.wait()


def pack(green_prev, energies, source, weight_index, table):
    width = green_prev.shape[-1]
    hbm, vmem = pl.BlockSpec(memory_space=pltpu.HBM), pl.BlockSpec(memory_space=pltpu.VMEM)
    return pl.pallas_call(
        pack_kernel,
        out_shape=[jax.ShapeDtypeStruct((width + ROWS, width), f32)] * 2,
        in_specs=[hbm] * 5,
        out_specs=[vmem] * 2,
        scratch_shapes=[
            pltpu.SMEM(energies.shape, f32), pltpu.SMEM(source.shape, jnp.int32),
            pltpu.SMEM(weight_index.shape, jnp.int32), pltpu.SMEM(table.shape, f32),
            pltpu.SemaphoreType.DMA((6,)),
        ],
        compiler_params=pltpu.CompilerParams(vmem_limit_bytes=40 * 2**20),
    )(energies, source, weight_index, table, green_prev)


def coef(rows, index):
    at = index.astype(f32)
    return jnp.where(rows[0:1] == at, rows[2:3], 0.0) + jnp.where(rows[1:2] == at, rows[3:4], 0.0)


def held(e):
    step = jnp.where(e % 2 == 0, 4, -4)
    other = e + 1 - 2 * (e % 2)
    return other, e - step, e + step, other + step, other - step


def over_x_kernel(re, twin_block, one, two, pair_one, pair_two, x, out):
    width = re.shape[1]
    e = lax.axis_index("energy")
    other, at_one, at_two, at_pair_one, at_pair_two = held(e)
    rows = x[width:]
    total = coef(rows, e) * re[:width] + coef(rows, other) * twin_block[0, 0, 0]
    total += coef(rows, at_one) * one[:width] + coef(rows, at_two) * two[:width]
    out[...] = total + coef(rows, at_pair_one) * pair_one[:width] + coef(rows, at_pair_two) * pair_two[:width]


def groups_kernel(im, twin_block, x, pair_x, near, one, two, out_1, out_2):
    width = im.shape[1]
    e = lax.axis_index("energy")
    other, at_one, at_two, _, _ = held(e)
    across = e + 2 - 4 * ((e // 2) % 2)
    pair_across = other + 2 - 4 * ((other // 2) % 2)
    for target, rows, out in ((at_two, two[width:], out_1), (at_one, one[width:], out_2)):
        upward = target > e
        near_index = jnp.where(upward, e - 1, e + 1)
        counts = e % 4 == jnp.where(upward, 0, 3)
        total = coef(rows, e) * im[:width] + coef(rows, other) * twin_block[0, 0, 1]
        total += coef(rows, across) * x[:width] + coef(rows, pair_across) * pair_x[:width]
        out[...] = total + jnp.where(counts, coef(rows, near_index), 0.0) * near[:width]


def own_kernel(re, im, twin_block, one, two, pair_one, pair_two, x, pair_x, ham, profile, coup, left, base_out, placed_out):
    width = re.shape[1]
    e = lax.axis_index("energy")
    other, at_one, at_two, at_pair_one, at_pair_two = held(e)
    across = e + 2 - 4 * ((e // 2) % 2)
    pair_across = other + 2 - 4 * ((other // 2) % 2)
    rows = re[width:]
    total = coef(rows, e) * re[:width] + coef(rows, other) * twin_block[0, 0, 0]
    total += coef(rows, at_one) * one[:width] + coef(rows, at_two) * two[:width]
    total += coef(rows, at_pair_one) * pair_one[:width] + coef(rows, at_pair_two) * pair_two[:width]
    unit = unit_of(width)
    base_out[0] = rows[4:5] * unit - ham[0] - profile[...] * total
    total = coef(rows, e) * im[:width] + coef(rows, other) * twin_block[0, 0, 1]
    total += coef(rows, across) * x[:width] + coef(rows, pair_across) * pair_x[:width]
    placed = mm(twice(one_hot(width, left[...]), 1), pair(coup[0], 1), NT)
    placed_out[...] = placed
    lead = jnp.where(lax.axis_index("slab") == 0, -0.5, 0.0) * mm(left3(placed), right3(placed, axis=1), NT)
    base_out[1] = BROAD * unit - profile[...] * total - lead


def first_kernel(own, re, profile, from_x, far, from_1, from_2, right, face_out, base_out):
    width, faces = profile.shape[0], right.shape[1]
    e = lax.axis_index("energy")
    weight = coef(re[width:], jnp.where(e % 4 == 3, e + SPAN, e - SPAN))
    base_re = own[0] - profile[...] * (from_x[...] + weight * far[:width])
    base_im = own[1] - profile[...] * (from_1[...] + from_2[...])
    base_out[0] = base_re
    base_out[1] = base_im

    @pl.when(lax.axis_index("slab") == 0)
    def _():
        f_re, f_im, _, _ = corner(base_re, base_im, one_hot(width, right[...]).astype(f32))
        face_out[:, :faces] = f_re
        face_out[:, faces:] = f_im


def bounded(base, placed, incoming):
    width, faces = placed.shape
    is_first = lax.axis_index("slab") == 0
    face = jnp.where(is_first, 0.0, incoming[...])
    split_placed = left3(placed[...])
    t = mm(split_placed, right3(face))
    bound = mm(stack(left3(t[:, :faces]), left3(t[:, faces:])), right3(placed[...], axis=1), NT)
    return base[0] - bound[:width], base[1] - bound[width:]


def face_kernel(base, placed, incoming, right, face_out):
    width, faces = placed.shape
    a_re, a_im = bounded(base, placed, incoming)
    f_re, f_im, _, _ = corner(a_re, a_im, one_hot(width, right[...]).astype(f32))
    face_out[:, :faces] = f_re
    face_out[:, faces:] = f_im


def face_parts(g_re, g_im, right, cols_out, rows_out):
    width = g_re.shape[0]
    hot = one_hot(width, right[...])
    high, low = split(both(g_re, g_im))
    cols_out[...] = mm(jnp.concatenate([high, low], axis=1), twice(hot, 0))
    wide_high = jnp.concatenate([high[:width], high[width:]], axis=1)
    wide_low = jnp.concatenate([low[:width], low[width:]], axis=1)
    rows_out[...] = mm(twice(hot.T, 1), stack(wide_high, wide_low))


def whole(a_re, a_im, right, g_out, cols_out, rows_out):
    e, q, scale = begin(a_re, a_im)
    g_re, g_im = full(a_re, a_im, *series_of(e, q), scale)
    g_out[0] = g_re
    g_out[1] = g_im
    face_parts(g_re, g_im, right, cols_out, rows_out)


def slab_0_kernel(base, right, g_out, cols_out, rows_out):
    @pl.when(lax.axis_index("slab") == 0)
    def _():
        whole(base[0], base[1], right, g_out, cols_out, rows_out)


def middle_kernel(slabs, base, placed, incoming, right, g, cols, rows, g_out, cols_out, rows_out):
    slab = lax.axis_index("slab")

    @pl.when((slab != 0) & (slab != slabs - 1))
    def _():
        a_re, a_im = bounded(base, placed, incoming)
        whole(a_re, a_im, right, g_out, cols_out, rows_out)

    @pl.when((slab == 0) | (slab == slabs - 1))
    def _():
        g_out[...] = g[...]
        cols_out[...] = cols[...]
        rows_out[...] = rows[...]


def turn_kernel(slabs, base, placed, incoming, message_out, series_out, a_out, scale_out):
    @pl.when(lax.axis_index("slab") == slabs - 1)
    def _():
        width, faces = placed.shape
        a_re, a_im = bounded(base, placed, incoming)
        m_re, m_im, series, scale = corner(a_re, a_im, placed[...])
        message_out[:, :faces] = m_re
        message_out[:, faces:] = m_im
        for k, part in enumerate(series):
            series_out[k] = part
        a_out[0] = a_re
        a_out[1] = a_im
        scale_out[0] = scale


def message_kernel(slabs, cols, rows, message, coup, left, right, base, message_out):
    width, faces = base.shape[1], coup.shape[1]
    hot = one_hot(width, right[...])
    f = mm(twice(hot.T, 1), pair(cols[...].reshape(2 * width, faces)[:width], 0))
    f_im = mm(twice(hot.T, 1), pair(cols[width:], 0))
    order = mm(one_hot(width, left[...]), hot, TN).astype(bf16)
    mixed = mm(pair(coup[0], 1), twice(order, 0))
    t_re, t_im = complex_mm(f, f_im, message[:, :faces], message[:, faces:])
    c_re, c_im = complex_mm(t_re, t_im, f, f_im)
    t = mm(left3(both(f + c_re, f_im + c_im)), right3(mixed, axis=1), NT)
    wide = jnp.concatenate([t[:faces], t[faces:]], axis=1)
    is_last = lax.axis_index("slab") == slabs - 1

    @pl.when(jnp.logical_not(is_last))
    def _():
        message_out[...] = mm(left3(mixed), right3(wide))

    @pl.when(is_last)
    def _():
        message_out[...] = message[...]


def last_full_kernel(slabs, scale, series, a_in, green_out, block, sems):
    @pl.when(lax.axis_index("slab") == slabs - 1)
    def _():
        e, s_e = series[0], unit_of(a_in.shape[1]) + series[0]
        for turn in range(1, DOUBLINGS - 1):
            e = series[turn]
            s_e = s_e + times(herm(s_e, skew(s_e)), herm(e, skew(e)))
        e = series[DOUBLINGS - 1]
        block[0], block[1] = full(a_in[0], a_in[1], s_e, skew(s_e), e, skew(e), scale[0])
        copies = [pltpu.make_async_copy(block.at[k], green_out.at[0, 0, k], sems.at[k]) for k in range(2)]
        for copy in copies:
            copy.start()
        for copy in copies:
            copy.wait()


def last_kernel(slabs, g, cols, rows, message, given, green_out, block, sems):
    @pl.when(lax.axis_index("slab") != slabs - 1)
    def _():
        width, faces = g.shape[1], message.shape[0]
        t_re, t_im = complex_mm(message[:, :faces], message[:, faces:], rows[:, :width], rows[:, width:])
        c_re, c_im = complex_mm(cols[:width], cols[width:], t_re, t_im)
        copies = []
        for k, change in enumerate((c_re, c_im)):
            block[k] = g[k] + change
            copies.append(pltpu.make_async_copy(block.at[k], green_out.at[0, 0, k], sems.at[k]))
            copies[k].start()
        for copy in copies:
            copy.wait()


def write_green(kernel, scalars, arrays, shape, given=None):
    smem, vmem, hbm = (pl.BlockSpec(memory_space=space) for space in (pltpu.SMEM, pltpu.VMEM, pltpu.HBM))
    more = [] if given is None else [given]
    inputs = len(scalars) + len(arrays)
    return pl.pallas_call(
        kernel,
        out_shape=jax.ShapeDtypeStruct(shape, f32),
        in_specs=[smem] * len(scalars) + [vmem] * len(arrays) + [hbm] * len(more),
        out_specs=hbm,
        scratch_shapes=[pltpu.VMEM(shape[2:], f32), pltpu.SemaphoreType.DMA((2,))],
        input_output_aliases={inputs: 0} if more else {},
        compiler_params=pltpu.CompilerParams(vmem_limit_bytes=40 * 2**20),
    )(*scalars, *arrays, *more)


def call(kernel, outs, scalars, *arrays, scalar_outs=()):
    smem = pl.BlockSpec(memory_space=pltpu.SMEM)
    vmem = pl.BlockSpec(memory_space=pltpu.VMEM)
    return pl.pallas_call(
        kernel,
        out_shape=[jax.ShapeDtypeStruct(shape, f32) for shape in (*outs, *scalar_outs)],
        in_specs=[smem] * len(scalars) + [vmem] * len(arrays),
        out_specs=[vmem] * len(outs) + [smem] * len(scalar_outs),
        compiler_params=pltpu.CompilerParams(vmem_limit_bytes=40 * 2**20),
    )(*scalars, *arrays)


def exchange(energies, hamiltonian, coupling, green_prev, profile, phonon_weights, source, weight_index, left_face):
    count = lax.axis_size("energy")
    width = green_prev.shape[-1]
    block = (width, width)
    all_twin, all_x = pairs_of(twin, count), pairs_of(over_x, count)
    all_1, all_2 = pairs_of(group_1, count), pairs_of(group_2, count)
    groups = count // 4
    near_pairs = [(4 * k, 4 * k - 1) for k in range(2, groups)] + [(4 * k + 3, 4 * k + 4) for k in range(groups - 2)]
    far_pairs = [p for k in range(1, groups - 1) for p in ((4 * k, 4 * k - 1), (4 * k + 3, 4 * k + 4))]
    pair = sent(green_prev, all_twin)
    im, re = pack(green_prev, energies, source, weight_index, phonon_weights)
    x = sent(im, all_x)
    one = sent(re, all_1)
    two = sent(re, all_2)
    near = sent(im, near_pairs)
    x, near = lax.optimization_barrier((x, near))
    pair_one = sent(one, all_twin)
    pair_two = sent(two, all_twin)
    pair_x = sent(x, all_twin)
    (over_x_sum,) = call(over_x_kernel, [block], [], re, pair, one, two, pair_one, pair_two, x)
    sum_1, sum_2 = call(
        groups_kernel, [block] * 2, [], im, pair, x, pair_x, near, one, two
    )
    two_later, sum_1, sum_2, over_x_sum = lax.optimization_barrier((two, sum_1, sum_2, over_x_sum))
    from_x = sent(over_x_sum, all_x)
    from_1 = sent(sum_1, all_1)
    from_2 = sent(sum_2, all_2)
    far = sent(two_later, far_pairs)
    own, placed = call(
        own_kernel, [(2, *block), (width, coupling.shape[1])], [],
        re, im, pair, one, two, pair_one, pair_two, x, pair_x, hamiltonian, profile, coupling, left_face,
    )
    return placed, (own, re, profile, from_x, far, from_1, from_2)


def passed_along(value, steps):
    count = lax.axis_size("slab")
    return lax.ppermute(value, "slab", [(start, (start + steps) % count) for start in range(count)])


def on_device(
    energies, hamiltonian, coupling, green_prev, profile, phonon_weights, source, weight_index, left_face, right_face,
):
    width, faces = hamiltonian.shape[1], coupling.shape[1]
    slabs = lax.axis_size("slab")
    block, face = (width, width), (faces, 2 * faces)
    parts_of_g = [(2, *block), (2 * width, faces), (faces, 2 * width)]
    placed, parts = exchange(
        energies, hamiltonian, coupling, green_prev, profile, phonon_weights, source, weight_index, left_face
    )
    face_sent, base = call(first_kernel, [face, (2, *block)], [], *parts, right_face)
    incoming = passed_along(face_sent, 1)
    for turn in range(1, slabs - 1):
        (face_sent,) = call(face_kernel, [face], [], base, placed, incoming, right_face)
        incoming = passed_along(face_sent, 1)
    g, cols, rows = call(slab_0_kernel, parts_of_g, [], base, right_face)
    placed, g = lax.optimization_barrier((placed, g))
    if slabs > 2:
        g, cols, rows = call(
            functools.partial(middle_kernel, slabs), parts_of_g, [], base, placed, incoming, right_face, g, cols, rows
        )
    message, series, a, scale = call(
        functools.partial(turn_kernel, slabs), [face, (4, *block), (2, *block)], [], base, placed, incoming,
        scalar_outs=[(1,)],
    )
    incoming = passed_along(message, -1)
    green = write_green(functools.partial(last_full_kernel, slabs), [scale], [series, a], green_prev.shape)
    for turn in range(2, slabs):
        (message,) = call(
            functools.partial(message_kernel, slabs), [face], [],
            cols, rows, incoming, coupling, left_face, right_face, base,
        )
        incoming = passed_along(message, -1)
    return write_green(functools.partial(last_kernel, slabs), [], [g, cols, rows, incoming], green_prev.shape, green)


def solution(mesh):
    in_specs = (
        P("energy"),
        P("slab", None, None),
        P("slab", None, None),
        P("energy", "slab", None, None, None),
        P(),
        P(),
        P("energy", None),
        P("energy", None),
        P("slab", None),
        P("slab", None),
    )
    out_specs = P("energy", "slab", None, None, None)
    return jax.shard_map(on_device, mesh=mesh, in_specs=in_specs, out_specs=out_specs, check_vma=False)
```

```python
import functools

import jax
import jax.numpy as jnp
from jax import lax
from jax.experimental import pallas as pl
from jax.experimental.pallas import tpu as pltpu
from jax.sharding import PartitionSpec as P

SPAN = 5
BROAD = 0.02
DOUBLINGS = 4

f32 = jnp.float32
bf16 = jnp.bfloat16
NN = (((1,), (0,)), ((), ()))
NT = (((1,), (1,)), ((), ()))
TN = (((0,), (0,)), ((), ()))


def split(x):
    high = x.astype(bf16)
    return high, (x - high.astype(f32)).astype(bf16)


def mm(a, b, dims=NN):
    return lax.dot_general(a, b, dims, preferred_element_type=f32)


def left3(*terms):
    out = []
    for x in terms:
        high, low = split(x)
        out += [high, high, low]
    return jnp.concatenate(out, axis=1)


def right3(*terms, axis=0):
    out = []
    for x in terms:
        high, low = split(x)
        out += [high, low, high]
    return jnp.concatenate(out, axis=axis)


def pair(x, axis):
    return jnp.concatenate(split(x), axis=axis)


def twice(x, axis):
    return jnp.concatenate([x, x], axis=axis)


def both(x_re, x_im):
    return jnp.concatenate([x_re, x_im], axis=0)


def skew(e):
    return 0.5 * (e - e.T)


def stack(*parts):
    return jnp.concatenate(parts, axis=0)


def left_of(high, low):
    return jnp.concatenate([high, high, low], axis=1)


def right_of(high, low):
    return jnp.concatenate([high, low, high], axis=0)


def herm(e, q):
    return split(e), split(q)


def times(s, h):
    return mm(left_of(*s[0]), right_of(*h[0])) - 2.0 * mm(left_of(*s[1]), right_of(*h[1]))


def rows_times(e_rows, q_rows, h):
    count = e_rows.shape[0]
    e_high, e_low = split(e_rows)
    q_high, q_low = split(q_rows)
    from_e = mm(stack(e_high, e_low), h[0][0])
    from_q = mm(stack(q_high, q_low), h[1][0])
    lows = mm(e_high, h[0][1]) + mm(q_high, h[1][1])
    return (from_e[:count] + from_e[count:]) + (from_q[:count] + from_q[count:]) + lows


def thin_times(y_re, y_im, h):
    out = rows_times(stack(y_re, y_im), stack(-(y_re + y_im), y_re - y_im), h)
    return out[:y_re.shape[0]], out[y_re.shape[0]:]


def complex_mm(a_re, a_im, b_re, b_im):
    rows = a_re.shape[0]
    out = mm(stack(left3(a_re, -a_im), left3(a_im, a_re)), right3(b_re, b_im))
    return out[:rows], out[rows:]


def one_hot(width, face):
    return (lax.broadcasted_iota(jnp.int32, (width, face.shape[1]), 0) == face).astype(bf16)


def unit_of(width):
    row = lax.broadcasted_iota(jnp.int32, (width, width), 0)
    return (row == lax.broadcasted_iota(jnp.int32, (width, width), 1)).astype(f32)


def begin(a_re, a_im):
    total = a_re + a_im
    gram = mm(left3(total), right3(total, axis=1), NT) - mm(left3(2.0 * a_re), right3(a_im, axis=1), NT)
    modulus = jnp.sqrt(a_re * a_re + a_im * a_im)
    col_norm = jnp.max(jnp.sum(modulus, axis=0))
    row_norm = jnp.max(jnp.sum(modulus, axis=1))
    scale = 1.0 / (col_norm * row_norm)
    return unit_of(a_re.shape[0]) - scale * gram, (-scale) * skew(gram), scale


def corner(a_re, a_im, proj):
    width, faces = proj.shape
    e, q, scale = begin(a_re, a_im)
    proj_t = proj.T
    y = scale * mm(left3(proj_t), right3(both(a_re, a_im), axis=1), NT)
    y_re, y_im = y[:, :width], -y[:, width:]
    powers = [e]
    for turn in range(1, DOUBLINGS):
        h = herm(e, q)
        e = times(h, h)
        q = skew(e)
        powers.append(e)
        c_re, c_im = thin_times(y_re, y_im, h)
        y_re, y_im = y_re + c_re, y_im + c_im
    h = herm(e, q)
    c_re, c_im = thin_times(y_re, y_im, h)
    y_re, y_im = y_re + c_re, y_im + c_im
    none = jnp.zeros_like(proj_t)
    t_re, t_im = thin_times(proj_t, none, h)
    u_re, u_im = thin_times(y_re, y_im, h)
    out = mm(left3(both(y_re, y_im)), right3(proj))
    out += mm(stack(left3(u_re, u_im), left3(u_im, -u_re)), right3(t_re, t_im, axis=1), NT)
    return out[:faces], out[faces:], powers, scale


def series_of(e, q):
    s_e, s_q = unit_of(e.shape[0]) + e, q
    for turn in range(1, DOUBLINGS):
        h = herm(e, q)
        if turn > 1:
            s_e = s_e + times(herm(s_e, s_q), h)
            s_q = skew(s_e)
        e = times(h, h)
        q = skew(e)
    return s_e, s_q, e, q


def full(a_re, a_im, s_e, s_q, e, q, store):
    h = herm(e, q)
    s_e = s_e + times(herm(s_e, s_q), h)
    e = times(h, h)
    s_e = s_e + times(herm(s_e, skew(s_e)), herm(e, skew(e)))
    s_q = skew(s_e)
    s_p = s_e - s_q
    b, c = a_re.T, a_im.T
    one = mm(left3(b - c), right3(s_p))
    store(0, one + mm(left3(c), right3(s_e)))
    store(1, one + mm(left3(b), right3(s_q - s_p)))


ROWS = 8


def over_x(e):
    return e ^ 2


def twin(e):
    return e ^ 1


def group_1(e):
    return e + 4 if e % 2 == 0 else e - 4


def group_2(e):
    return e - 4 if e % 2 == 0 else e + 4


def sent(value, pairs):
    return lax.ppermute(value, "energy", pairs)


def pairs_of(target, count):
    return [(e, target(e)) for e in range(count) if 0 <= target(e) < count]


def pack_kernel(energy_hbm, source_hbm, index_hbm, table_hbm, green, im_out, re_out, energy, source, index, table, sems):
    width = green.shape[3]
    copies = [
        pltpu.make_async_copy(start, end, sems.at[k])
        for k, (start, end) in enumerate((
            (energy_hbm, energy), (source_hbm, source), (index_hbm, index), (table_hbm, table),
            (green.at[0, 0, 1], im_out.at[pl.ds(0, width)]), (green.at[0, 0, 0], re_out.at[pl.ds(0, width)]),
        ))
    ]
    for copy in copies:
        copy.start()
    for copy in copies[:4]:
        copy.wait()
    row = lax.broadcasted_iota(jnp.int32, (ROWS, width), 0)
    rows = jnp.where(row == 4, energy[0], 0.0)
    for term in range(2):
        rows = jnp.where(row == term, source[0, term].astype(f32), rows)
        rows = jnp.where(row == 2 + term, table[index[0, term]], rows)
    im_out[width:] = rows
    re_out[width:] = rows
    for copy in copies[4:]:
        copy.wait()


def pack(green_prev, energies, source, weight_index, table):
    width = green_prev.shape[-1]
    hbm, vmem = pl.BlockSpec(memory_space=pltpu.HBM), pl.BlockSpec(memory_space=pltpu.VMEM)
    return pl.pallas_call(
        pack_kernel,
        out_shape=[jax.ShapeDtypeStruct((width + ROWS, width), f32)] * 2,
        in_specs=[hbm] * 5,
        out_specs=[vmem] * 2,
        scratch_shapes=[
            pltpu.SMEM(energies.shape, f32), pltpu.SMEM(source.shape, jnp.int32),
            pltpu.SMEM(weight_index.shape, jnp.int32), pltpu.SMEM(table.shape, f32),
            pltpu.SemaphoreType.DMA((6,)),
        ],
        compiler_params=pltpu.CompilerParams(vmem_limit_bytes=40 * 2**20),
    )(energies, source, weight_index, table, pltpu.with_memory_space_constraint(green_prev, pltpu.HBM))


def coef(rows, index):
    at = index.astype(f32)
    return jnp.where(rows[0:1] == at, rows[2:3], 0.0) + jnp.where(rows[1:2] == at, rows[3:4], 0.0)


def held(e):
    step = jnp.where(e % 2 == 0, 4, -4)
    other = e + 1 - 2 * (e % 2)
    return other, e - step, e + step, other + step, other - step


def over_x_kernel(re, twin_block, one, two, pair_one, pair_two, x, out):
    width = re.shape[1]
    e = lax.axis_index("energy")
    other, at_one, at_two, at_pair_one, at_pair_two = held(e)
    rows = x[width:]
    total = coef(rows, e) * re[:width] + coef(rows, other) * twin_block[0, 0, 0]
    total += coef(rows, at_one) * one[:width] + coef(rows, at_two) * two[:width]
    out[...] = total + coef(rows, at_pair_one) * pair_one[:width] + coef(rows, at_pair_two) * pair_two[:width]


def groups_kernel(im, twin_block, x, pair_x, near, one, two, out_1, out_2):
    width = im.shape[1]
    e = lax.axis_index("energy")
    other, at_one, at_two, _, _ = held(e)
    across = e + 2 - 4 * ((e // 2) % 2)
    pair_across = other + 2 - 4 * ((other // 2) % 2)
    for target, rows, out in ((at_two, two[width:], out_1), (at_one, one[width:], out_2)):
        upward = target > e
        near_index = jnp.where(upward, e - 1, e + 1)
        counts = e % 4 == jnp.where(upward, 0, 3)
        total = coef(rows, e) * im[:width] + coef(rows, other) * twin_block[0, 0, 1]
        total += coef(rows, across) * x[:width] + coef(rows, pair_across) * pair_x[:width]
        out[...] = total + jnp.where(counts, coef(rows, near_index), 0.0) * near[:width]


def own_kernel(re, im, twin_block, one, two, pair_one, pair_two, x, pair_x, ham, profile, coup, left, base_out, placed_out):
    width = re.shape[1]
    e = lax.axis_index("energy")
    other, at_one, at_two, at_pair_one, at_pair_two = held(e)
    across = e + 2 - 4 * ((e // 2) % 2)
    pair_across = other + 2 - 4 * ((other // 2) % 2)
    rows = re[width:]
    total = coef(rows, e) * re[:width] + coef(rows, other) * twin_block[0, 0, 0]
    total += coef(rows, at_one) * one[:width] + coef(rows, at_two) * two[:width]
    total += coef(rows, at_pair_one) * pair_one[:width] + coef(rows, at_pair_two) * pair_two[:width]
    unit = unit_of(width)
    base_out[0] = rows[4:5] * unit - ham[0] - profile[...] * total
    total = coef(rows, e) * im[:width] + coef(rows, other) * twin_block[0, 0, 1]
    total += coef(rows, across) * x[:width] + coef(rows, pair_across) * pair_x[:width]
    placed = mm(twice(one_hot(width, left[...]), 1), pair(coup[0], 1), NT)
    placed_out[...] = placed
    lead = jnp.where(lax.axis_index("slab") == 0, -0.5, 0.0) * mm(left3(placed), right3(placed, axis=1), NT)
    base_out[1] = BROAD * unit - profile[...] * total - lead


def first_kernel(own, re, profile, from_x, far, from_1, from_2, right, face_out, base_out):
    width, faces = profile.shape[0], right.shape[1]
    e = lax.axis_index("energy")
    weight = coef(re[width:], jnp.where(e % 4 == 3, e + SPAN, e - SPAN))
    base_re = own[0] - profile[...] * (from_x[...] + weight * far[:width])
    base_im = own[1] - profile[...] * (from_1[...] + from_2[...])
    base_out[0] = base_re
    base_out[1] = base_im

    @pl.when(lax.axis_index("slab") == 0)
    def _():
        f_re, f_im, _, _ = corner(base_re, base_im, one_hot(width, right[...]).astype(f32))
        face_out[:, :faces] = f_re
        face_out[:, faces:] = f_im


def bounded(base, placed, incoming):
    width, faces = placed.shape
    is_first = lax.axis_index("slab") == 0
    face = jnp.where(is_first, 0.0, incoming[...])
    split_placed = left3(placed[...])
    t = mm(split_placed, right3(face))
    bound = mm(stack(left3(t[:, :faces]), left3(t[:, faces:])), right3(placed[...], axis=1), NT)
    return base[0] - bound[:width], base[1] - bound[width:]


def face_kernel(base, placed, incoming, right, face_out):
    width, faces = placed.shape
    a_re, a_im = bounded(base, placed, incoming)
    f_re, f_im, _, _ = corner(a_re, a_im, one_hot(width, right[...]).astype(f32))
    face_out[:, :faces] = f_re
    face_out[:, faces:] = f_im


def face_parts(g_re, g_im, right, cols_out, rows_out):
    width = g_re.shape[0]
    hot = one_hot(width, right[...])
    high, low = split(both(g_re, g_im))
    cols_out[...] = mm(jnp.concatenate([high, low], axis=1), twice(hot, 0))
    wide_high = jnp.concatenate([high[:width], high[width:]], axis=1)
    wide_low = jnp.concatenate([low[:width], low[width:]], axis=1)
    rows_out[...] = mm(twice(hot.T, 1), stack(wide_high, wide_low))


def whole(a_re, a_im, right, g_out, cols_out, rows_out):
    e, q, scale = begin(a_re, a_im)

    def store(k, part):
        g_out[k] = part

    full(scale * a_re, scale * a_im, *series_of(e, q), store)
    face_parts(g_out[0], g_out[1], right, cols_out, rows_out)


def slab_0_kernel(base, right, g_out, cols_out, rows_out):
    @pl.when(lax.axis_index("slab") == 0)
    def _():
        whole(base[0], base[1], right, g_out, cols_out, rows_out)


def middle_kernel(slabs, base, placed, incoming, right, g, cols, rows, g_out, cols_out, rows_out):
    slab = lax.axis_index("slab")

    @pl.when((slab != 0) & (slab != slabs - 1))
    def _():
        a_re, a_im = bounded(base, placed, incoming)
        whole(a_re, a_im, right, g_out, cols_out, rows_out)

    @pl.when((slab == 0) | (slab == slabs - 1))
    def _():
        g_out[...] = g[...]
        cols_out[...] = cols[...]
        rows_out[...] = rows[...]


def turn_kernel(slabs, base, placed, incoming, message_out, series_out, a_out):
    @pl.when(lax.axis_index("slab") == slabs - 1)
    def _():
        width, faces = placed.shape
        a_re, a_im = bounded(base, placed, incoming)
        m_re, m_im, series, scale = corner(a_re, a_im, placed[...])
        message_out[:, :faces] = m_re
        message_out[:, faces:] = m_im
        for k, part in enumerate(series):
            series_out[k] = part
        a_out[0] = scale * a_re
        a_out[1] = scale * a_im


def message_kernel(slabs, cols, rows, message, coup, left, right, base, message_out):
    width, faces = base.shape[1], coup.shape[1]
    hot = one_hot(width, right[...])
    f = mm(twice(hot.T, 1), pair(cols[...].reshape(2 * width, faces)[:width], 0))
    f_im = mm(twice(hot.T, 1), pair(cols[width:], 0))
    order = mm(one_hot(width, left[...]), hot, TN).astype(bf16)
    mixed = mm(pair(coup[0], 1), twice(order, 0))
    t_re, t_im = complex_mm(f, f_im, message[:, :faces], message[:, faces:])
    c_re, c_im = complex_mm(t_re, t_im, f, f_im)
    t = mm(left3(both(f + c_re, f_im + c_im)), right3(mixed, axis=1), NT)
    wide = jnp.concatenate([t[:faces], t[faces:]], axis=1)
    is_last = lax.axis_index("slab") == slabs - 1

    @pl.when(jnp.logical_not(is_last))
    def _():
        message_out[...] = mm(left3(mixed), right3(wide))

    @pl.when(is_last)
    def _():
        message_out[...] = message[...]


def last_full_kernel(slabs, series, scaled, green_out, block, sems):
    @pl.when(lax.axis_index("slab") == slabs - 1)
    def _():
        e, s_e = series[0], unit_of(scaled.shape[1]) + series[0]
        for turn in range(1, DOUBLINGS - 1):
            e = series[turn]
            s_e = s_e + times(herm(s_e, skew(s_e)), herm(e, skew(e)))
        e = series[DOUBLINGS - 1]
        copies = [pltpu.make_async_copy(block.at[k], green_out.at[0, 0, k], sems.at[k]) for k in range(2)]

        def store(k, part):
            block[k] = part
            copies[k].start()

        full(scaled[0], scaled[1], s_e, skew(s_e), e, skew(e), store)
        for copy in copies:
            copy.wait()


def last_kernel(slabs, g, cols, rows, message, given, green_out, block, sems):
    @pl.when(lax.axis_index("slab") != slabs - 1)
    def _():
        width, faces = g.shape[1], message.shape[0]
        t_re, t_im = complex_mm(message[:, :faces], message[:, faces:], rows[:, :width], rows[:, width:])
        c_re, c_im = complex_mm(cols[:width], cols[width:], t_re, t_im)
        copies = []
        for k, change in enumerate((c_re, c_im)):
            block[k] = g[k] + change
            copies.append(pltpu.make_async_copy(block.at[k], green_out.at[0, 0, k], sems.at[k]))
            copies[k].start()
        for copy in copies:
            copy.wait()


def write_green(kernel, arrays, shape, given=None):
    vmem, hbm = (pl.BlockSpec(memory_space=space) for space in (pltpu.VMEM, pltpu.HBM))
    more = [] if given is None else [given]
    return pl.pallas_call(
        kernel,
        out_shape=jax.ShapeDtypeStruct(shape, f32),
        in_specs=[vmem] * len(arrays) + [hbm] * len(more),
        out_specs=hbm,
        scratch_shapes=[pltpu.VMEM(shape[2:], f32), pltpu.SemaphoreType.DMA((2,))],
        input_output_aliases={len(arrays): 0} if more else {},
        compiler_params=pltpu.CompilerParams(vmem_limit_bytes=40 * 2**20),
    )(*arrays, *more)


def call(kernel, outs, *arrays):
    vmem = pl.BlockSpec(memory_space=pltpu.VMEM)
    return pl.pallas_call(
        kernel,
        out_shape=[jax.ShapeDtypeStruct(shape, f32) for shape in outs],
        in_specs=[vmem] * len(arrays),
        out_specs=[vmem] * len(outs),
        compiler_params=pltpu.CompilerParams(vmem_limit_bytes=40 * 2**20),
    )(*arrays)


def exchange(energies, hamiltonian, coupling, green_prev, profile, phonon_weights, source, weight_index, left_face):
    count = lax.axis_size("energy")
    width = green_prev.shape[-1]
    block = (width, width)
    all_twin, all_x = pairs_of(twin, count), pairs_of(over_x, count)
    all_1, all_2 = pairs_of(group_1, count), pairs_of(group_2, count)
    groups = count // 4
    near_pairs = [(4 * k, 4 * k - 1) for k in range(2, groups)] + [(4 * k + 3, 4 * k + 4) for k in range(groups - 2)]
    far_pairs = [p for k in range(1, groups - 1) for p in ((4 * k, 4 * k - 1), (4 * k + 3, 4 * k + 4))]
    pair = sent(green_prev, all_twin)
    im, re = pack(green_prev, energies, source, weight_index, phonon_weights)
    x = sent(im, all_x)
    one = sent(re, all_1)
    two = sent(re, all_2)
    near = sent(im, near_pairs)
    x, near = lax.optimization_barrier((x, near))
    pair_one = sent(one, all_twin)
    pair_two = sent(two, all_twin)
    pair_x = sent(x, all_twin)
    (over_x_sum,) = call(over_x_kernel, [block], re, pair, one, two, pair_one, pair_two, x)
    sum_1, sum_2 = call(
        groups_kernel, [block] * 2, im, pair, x, pair_x, near, one, two
    )
    two_later, sum_1, sum_2, over_x_sum = lax.optimization_barrier((two, sum_1, sum_2, over_x_sum))
    from_x = sent(over_x_sum, all_x)
    from_1 = sent(sum_1, all_1)
    from_2 = sent(sum_2, all_2)
    far = sent(two_later, far_pairs)
    own, placed = call(
        own_kernel, [(2, *block), (width, coupling.shape[1])],
        re, im, pair, one, two, pair_one, pair_two, x, pair_x, hamiltonian, profile, coupling, left_face,
    )
    return placed, (own, re, profile, from_x, far, from_1, from_2)


def passed_along(value, steps):
    count = lax.axis_size("slab")
    return lax.ppermute(value, "slab", [(start, (start + steps) % count) for start in range(count)])


def on_device(
    energies, hamiltonian, coupling, green_prev, profile, phonon_weights, source, weight_index, left_face, right_face,
):
    width, faces = hamiltonian.shape[1], coupling.shape[1]
    slabs = lax.axis_size("slab")
    block, face = (width, width), (faces, 2 * faces)
    parts_of_g = [(2, *block), (2 * width, faces), (faces, 2 * width)]
    placed, parts = exchange(
        energies, hamiltonian, coupling, green_prev, profile, phonon_weights, source, weight_index, left_face
    )
    face_sent, base = call(first_kernel, [face, (2, *block)], *parts, right_face)
    incoming = passed_along(face_sent, 1)
    for turn in range(1, slabs - 1):
        (face_sent,) = call(face_kernel, [face], base, placed, incoming, right_face)
        incoming = passed_along(face_sent, 1)
    g, cols, rows = call(slab_0_kernel, parts_of_g, base, right_face)
    placed, g = lax.optimization_barrier((placed, g))
    if slabs > 2:
        g, cols, rows = call(
            functools.partial(middle_kernel, slabs), parts_of_g, base, placed, incoming, right_face, g, cols, rows
        )
    message, series, scaled = call(
        functools.partial(turn_kernel, slabs), [face, (DOUBLINGS, *block), (2, *block)], base, placed, incoming
    )
    incoming = passed_along(message, -1)
    green = write_green(functools.partial(last_full_kernel, slabs), [series, scaled], green_prev.shape)
    for turn in range(2, slabs):
        (message,) = call(
            functools.partial(message_kernel, slabs), [face],
            cols, rows, incoming, coupling, left_face, right_face, base,
        )
        incoming = passed_along(message, -1)
    return write_green(functools.partial(last_kernel, slabs), [g, cols, rows, incoming], green_prev.shape, green)


def solution(mesh):
    in_specs = (
        P("energy"),
        P("slab", None, None),
        P("slab", None, None),
        P("energy", "slab", None, None, None),
        P(),
        P(),
        P("energy", None),
        P("energy", None),
        P("slab", None),
        P("slab", None),
    )
    out_specs = P("energy", "slab", None, None, None)
    return jax.shard_map(on_device, mesh=mesh, in_specs=in_specs, out_specs=out_specs, check_vma=False)
```

```python
import functools

import jax
import jax.numpy as jnp
from jax import lax
from jax.experimental import pallas as pl
from jax.experimental.pallas import tpu as pltpu
from jax.sharding import PartitionSpec as P

SPAN = 5
BROAD = 0.02
DOUBLINGS = 4

f32 = jnp.float32
bf16 = jnp.bfloat16
NN = (((1,), (0,)), ((), ()))
NT = (((1,), (1,)), ((), ()))
TN = (((0,), (0,)), ((), ()))


def split(x):
    high = x.astype(bf16)
    return high, (x - high.astype(f32)).astype(bf16)


def mm(a, b, dims=NN):
    return lax.dot_general(a, b, dims, preferred_element_type=f32)


def left3(*terms):
    out = []
    for x in terms:
        high, low = split(x)
        out += [high, high, low]
    return jnp.concatenate(out, axis=1)


def right3(*terms, axis=0):
    out = []
    for x in terms:
        high, low = split(x)
        out += [high, low, high]
    return jnp.concatenate(out, axis=axis)


def pair(x, axis):
    return jnp.concatenate(split(x), axis=axis)


def twice(x, axis):
    return jnp.concatenate([x, x], axis=axis)


def both(x_re, x_im):
    return jnp.concatenate([x_re, x_im], axis=0)


def skew(e):
    return 0.5 * (e - e.T)


def stack(*parts):
    return jnp.concatenate(parts, axis=0)


def left_of(high, low):
    return jnp.concatenate([high, high, low], axis=1)


def right_of(high, low):
    return jnp.concatenate([high, low, high], axis=0)


def herm(e, q):
    return split(e), split(q)


def times(s, h):
    return mm(left_of(*s[0]), right_of(*h[0])) - 2.0 * mm(left_of(*s[1]), right_of(*h[1]))


def rows_times(e_rows, q_rows, h):
    count = e_rows.shape[0]
    e_high, e_low = split(e_rows)
    q_high, q_low = split(q_rows)
    from_e = mm(stack(e_high, e_low), h[0][0])
    from_q = mm(stack(q_high, q_low), h[1][0])
    lows = mm(e_high, h[0][1]) + mm(q_high, h[1][1])
    return (from_e[:count] + from_e[count:]) + (from_q[:count] + from_q[count:]) + lows


def thin_times(y_re, y_im, h):
    out = rows_times(stack(y_re, y_im), stack(-(y_re + y_im), y_re - y_im), h)
    return out[:y_re.shape[0]], out[y_re.shape[0]:]


def complex_mm(a_re, a_im, b_re, b_im):
    rows = a_re.shape[0]
    out = mm(stack(left3(a_re, -a_im), left3(a_im, a_re)), right3(b_re, b_im))
    return out[:rows], out[rows:]


def one_hot(width, face):
    return (lax.broadcasted_iota(jnp.int32, (width, face.shape[1]), 0) == face).astype(bf16)


def unit_of(width):
    row = lax.broadcasted_iota(jnp.int32, (width, width), 0)
    return (row == lax.broadcasted_iota(jnp.int32, (width, width), 1)).astype(f32)


def begin(a_re, a_im):
    total = a_re + a_im
    gram = mm(left3(total), right3(total, axis=1), NT) - mm(left3(2.0 * a_re), right3(a_im, axis=1), NT)
    modulus = jnp.sqrt(a_re * a_re + a_im * a_im)
    col_norm = jnp.max(jnp.sum(modulus, axis=0))
    row_norm = jnp.max(jnp.sum(modulus, axis=1))
    scale = 1.0 / (col_norm * row_norm)
    return unit_of(a_re.shape[0]) - scale * gram, (-scale) * skew(gram), scale


def corner(a_re, a_im, proj):
    width, faces = proj.shape
    e, q, scale = begin(a_re, a_im)
    proj_t = proj.T
    y = scale * mm(left3(proj_t), right3(both(a_re, a_im), axis=1), NT)
    y_re, y_im = y[:, :width], -y[:, width:]
    powers = [e]
    for turn in range(1, DOUBLINGS):
        h = herm(e, q)
        e = times(h, h)
        q = skew(e)
        powers.append(e)
        c_re, c_im = thin_times(y_re, y_im, h)
        y_re, y_im = y_re + c_re, y_im + c_im
    h = herm(e, q)
    c_re, c_im = thin_times(y_re, y_im, h)
    y_re, y_im = y_re + c_re, y_im + c_im
    none = jnp.zeros_like(proj_t)
    t_re, t_im = thin_times(proj_t, none, h)
    u_re, u_im = thin_times(y_re, y_im, h)
    out = mm(left3(both(y_re, y_im)), right3(proj))
    out += mm(stack(left3(u_re, u_im), left3(u_im, -u_re)), right3(t_re, t_im, axis=1), NT)
    return out[:faces], out[faces:], powers, scale


def series_of(e, q):
    s_e, s_q = unit_of(e.shape[0]) + e, q
    for turn in range(1, DOUBLINGS):
        h = herm(e, q)
        if turn > 1:
            s_e = s_e + times(herm(s_e, s_q), h)
            s_q = skew(s_e)
        e = times(h, h)
        q = skew(e)
    return s_e, s_q, e, q


def full(a_re, a_im, s_e, s_q, e, q, store):
    h = herm(e, q)
    s_e = s_e + times(herm(s_e, s_q), h)
    e = times(h, h)
    s_e = s_e + times(herm(s_e, skew(s_e)), herm(e, skew(e)))
    s_q = skew(s_e)
    s_p = s_e - s_q
    b, c = a_re.T, a_im.T
    one = mm(left3(b - c), right3(s_p))
    store(0, one + mm(left3(c), right3(s_e)))
    store(1, one + mm(left3(b), right3(s_q - s_p)))


ROWS = 8


def over_x(e):
    return e ^ 2


def twin(e):
    return e ^ 1


def group_1(e):
    return e + 4 if e % 2 == 0 else e - 4


def group_2(e):
    return e - 4 if e % 2 == 0 else e + 4


def sent(value, pairs):
    return lax.ppermute(value, "energy", pairs)


def pairs_of(target, count):
    return [(e, target(e)) for e in range(count) if 0 <= target(e) < count]


def pack_kernel(energy_hbm, source_hbm, index_hbm, table_hbm, green, im_out, re_out, energy, source, index, table, sems):
    width = green.shape[3]
    copies = [
        pltpu.make_async_copy(start, end, sems.at[k])
        for k, (start, end) in enumerate((
            (energy_hbm, energy), (source_hbm, source), (index_hbm, index), (table_hbm, table),
            (green.at[0, 0, 1], im_out.at[pl.ds(0, width)]), (green.at[0, 0, 0], re_out.at[pl.ds(0, width)]),
        ))
    ]
    for copy in copies:
        copy.start()
    for copy in copies[:4]:
        copy.wait()
    row = lax.broadcasted_iota(jnp.int32, (ROWS, width), 0)
    rows = jnp.where(row == 4, energy[0], 0.0)
    for term in range(2):
        rows = jnp.where(row == term, source[0, term].astype(f32), rows)
        rows = jnp.where(row == 2 + term, table[index[0, term]], rows)
    im_out[width:] = rows
    re_out[width:] = rows
    for copy in copies[4:]:
        copy.wait()


def pack(green_prev, energies, source, weight_index, table):
    width = green_prev.shape[-1]
    hbm, vmem = pl.BlockSpec(memory_space=pltpu.HBM), pl.BlockSpec(memory_space=pltpu.VMEM)
    return pl.pallas_call(
        pack_kernel,
        out_shape=[jax.ShapeDtypeStruct((width + ROWS, width), f32)] * 2,
        in_specs=[hbm] * 5,
        out_specs=[vmem] * 2,
        scratch_shapes=[
            pltpu.SMEM(energies.shape, f32), pltpu.SMEM(source.shape, jnp.int32),
            pltpu.SMEM(weight_index.shape, jnp.int32), pltpu.SMEM(table.shape, f32),
            pltpu.SemaphoreType.DMA((6,)),
        ],
        compiler_params=pltpu.CompilerParams(vmem_limit_bytes=40 * 2**20),
    )(energies, source, weight_index, table, pltpu.with_memory_space_constraint(green_prev, pltpu.HBM))


def coef(rows, index):
    at = index.astype(f32)
    return jnp.where(rows[0:1] == at, rows[2:3], 0.0) + jnp.where(rows[1:2] == at, rows[3:4], 0.0)


def held(e):
    step = jnp.where(e % 2 == 0, 4, -4)
    other = e + 1 - 2 * (e % 2)
    return other, e - step, e + step, other + step, other - step


def over_x_kernel(re, twin_block, one, two, pair_one, pair_two, x, out):
    width = re.shape[1]
    e = lax.axis_index("energy")
    other, at_one, at_two, at_pair_one, at_pair_two = held(e)
    rows = x[width:]
    total = coef(rows, e) * re[:width] + coef(rows, other) * twin_block[0, 0, 0]
    total += coef(rows, at_one) * one[:width] + coef(rows, at_two) * two[:width]
    out[...] = total + coef(rows, at_pair_one) * pair_one[:width] + coef(rows, at_pair_two) * pair_two[:width]


def groups_kernel(im, twin_block, x, pair_x, near, one, two, out_1, out_2):
    width = im.shape[1]
    e = lax.axis_index("energy")
    other, at_one, at_two, _, _ = held(e)
    across = e + 2 - 4 * ((e // 2) % 2)
    pair_across = other + 2 - 4 * ((other // 2) % 2)
    for target, rows, out in ((at_two, two[width:], out_1), (at_one, one[width:], out_2)):
        upward = target > e
        near_index = jnp.where(upward, e - 1, e + 1)
        counts = e % 4 == jnp.where(upward, 0, 3)
        total = coef(rows, e) * im[:width] + coef(rows, other) * twin_block[0, 0, 1]
        total += coef(rows, across) * x[:width] + coef(rows, pair_across) * pair_x[:width]
        out[...] = total + jnp.where(counts, coef(rows, near_index), 0.0) * near[:width]


def own_kernel(re, im, twin_block, one, two, pair_one, pair_two, x, pair_x, ham, profile, coup, left, base_out, placed_out):
    width = re.shape[1]
    e = lax.axis_index("energy")
    other, at_one, at_two, at_pair_one, at_pair_two = held(e)
    across = e + 2 - 4 * ((e // 2) % 2)
    pair_across = other + 2 - 4 * ((other // 2) % 2)
    rows = re[width:]
    total = coef(rows, e) * re[:width] + coef(rows, other) * twin_block[0, 0, 0]
    total += coef(rows, at_one) * one[:width] + coef(rows, at_two) * two[:width]
    total += coef(rows, at_pair_one) * pair_one[:width] + coef(rows, at_pair_two) * pair_two[:width]
    unit = unit_of(width)
    base_out[0] = rows[4:5] * unit - ham[0] - profile[...] * total
    total = coef(rows, e) * im[:width] + coef(rows, other) * twin_block[0, 0, 1]
    total += coef(rows, across) * x[:width] + coef(rows, pair_across) * pair_x[:width]
    placed = mm(twice(one_hot(width, left[...]), 1), pair(coup[0], 1), NT)
    placed_out[...] = placed
    lead = jnp.where(lax.axis_index("slab") == 0, -0.5, 0.0) * mm(left3(placed), right3(placed, axis=1), NT)
    base_out[1] = BROAD * unit - profile[...] * total - lead


def first_kernel(own, re, profile, from_x, far, from_1, from_2, right, face_out, base_out):
    width, faces = profile.shape[0], right.shape[1]
    e = lax.axis_index("energy")
    weight = coef(re[width:], jnp.where(e % 4 == 3, e + SPAN, e - SPAN))
    base_re = own[0] - profile[...] * (from_x[...] + weight * far[:width])
    base_im = own[1] - profile[...] * (from_1[...] + from_2[...])
    base_out[0] = base_re
    base_out[1] = base_im

    @pl.when(lax.axis_index("slab") == 0)
    def _():
        f_re, f_im, _, _ = corner(base_re, base_im, one_hot(width, right[...]).astype(f32))
        face_out[:, :faces] = f_re
        face_out[:, faces:] = f_im


def bounded(base, placed, incoming):
    width, faces = placed.shape
    is_first = lax.axis_index("slab") == 0
    face = jnp.where(is_first, 0.0, incoming[...])
    split_placed = left3(placed[...])
    t = mm(split_placed, right3(face))
    bound = mm(stack(left3(t[:, :faces]), left3(t[:, faces:])), right3(placed[...], axis=1), NT)
    return base[0] - bound[:width], base[1] - bound[width:]


def face_kernel(base, placed, incoming, right, face_out):
    width, faces = placed.shape
    a_re, a_im = bounded(base, placed, incoming)
    f_re, f_im, _, _ = corner(a_re, a_im, one_hot(width, right[...]).astype(f32))
    face_out[:, :faces] = f_re
    face_out[:, faces:] = f_im


def face_parts(g_re, g_im, right, cols_out, rows_out):
    width = g_re.shape[0]
    hot = one_hot(width, right[...])
    high, low = split(both(g_re, g_im))
    cols_out[...] = mm(jnp.concatenate([high, low], axis=1), twice(hot, 0))
    wide_high = jnp.concatenate([high[:width], high[width:]], axis=1)
    wide_low = jnp.concatenate([low[:width], low[width:]], axis=1)
    rows_out[...] = mm(twice(hot.T, 1), stack(wide_high, wide_low))


def whole(a_re, a_im, right, g_out, cols_out, rows_out):
    e, q, scale = begin(a_re, a_im)

    def store(k, part):
        g_out[k] = part

    full(scale * a_re, scale * a_im, *series_of(e, q), store)
    face_parts(g_out[0], g_out[1], right, cols_out, rows_out)


def slab_0_kernel(base, right, g_out, cols_out, rows_out):
    @pl.when(lax.axis_index("slab") == 0)
    def _():
        whole(base[0], base[1], right, g_out, cols_out, rows_out)


def middle_kernel(slabs, base, placed, incoming, right, g, cols, rows, g_out, cols_out, rows_out):
    slab = lax.axis_index("slab")

    @pl.when((slab != 0) & (slab != slabs - 1))
    def _():
        a_re, a_im = bounded(base, placed, incoming)
        whole(a_re, a_im, right, g_out, cols_out, rows_out)

    @pl.when((slab == 0) | (slab == slabs - 1))
    def _():
        g_out[...] = g[...]
        cols_out[...] = cols[...]
        rows_out[...] = rows[...]


def turn_kernel(slabs, base, placed, incoming, message_out, series_out, a_out):
    @pl.when(lax.axis_index("slab") == slabs - 1)
    def _():
        width, faces = placed.shape
        a_re, a_im = bounded(base, placed, incoming)
        m_re, m_im, series, scale = corner(a_re, a_im, placed[...])
        message_out[:, :faces] = m_re
        message_out[:, faces:] = m_im
        for k, part in enumerate(series):
            series_out[k] = part
        a_out[0] = scale * a_re
        a_out[1] = scale * a_im


def message_kernel(slabs, cols, message, own, coup, left, right, base, message_out):
    width, faces = base.shape[1], coup.shape[1]
    hot = one_hot(width, right[...])
    f = mm(twice(hot.T, 1), pair(cols[:width], 0))
    f_im = mm(twice(hot.T, 1), pair(cols[width:], 0))
    order = mm(one_hot(width, left[...]), hot, TN).astype(bf16)
    mixed = mm(pair(coup[0], 1), twice(order, 0))
    t_re, t_im = complex_mm(f, f_im, message[:, :faces], message[:, faces:])
    c_re, c_im = complex_mm(t_re, t_im, f, f_im)
    t = mm(left3(both(f + c_re, f_im + c_im)), right3(mixed, axis=1), NT)
    wide = jnp.concatenate([t[:faces], t[faces:]], axis=1)
    is_last = lax.axis_index("slab") == slabs - 1

    @pl.when(jnp.logical_not(is_last))
    def _():
        message_out[...] = mm(left3(mixed), right3(wide))

    @pl.when(is_last)
    def _():
        message_out[...] = own[...]


def last_full_kernel(slabs, series, scaled, green_out, block, sems):
    @pl.when(lax.axis_index("slab") == slabs - 1)
    def _():
        e, s_e = series[0], unit_of(scaled.shape[1]) + series[0]
        for turn in range(1, DOUBLINGS - 1):
            e = series[turn]
            s_e = s_e + times(herm(s_e, skew(s_e)), herm(e, skew(e)))
        e = series[DOUBLINGS - 1]
        copies = [pltpu.make_async_copy(block.at[k], green_out.at[0, 0, k], sems.at[k]) for k in range(2)]

        def store(k, part):
            block[k] = part
            copies[k].start()

        full(scaled[0], scaled[1], s_e, skew(s_e), e, skew(e), store)
        for copy in copies:
            copy.wait()


def last_kernel(slabs, g, cols, rows, message, given, green_out, block, sems):
    @pl.when(lax.axis_index("slab") != slabs - 1)
    def _():
        width, faces = g.shape[1], message.shape[0]
        t_re, t_im = complex_mm(message[:, :faces], message[:, faces:], rows[:, :width], rows[:, width:])
        c_re, c_im = complex_mm(cols[:width], cols[width:], t_re, t_im)
        copies = []
        for k, change in enumerate((c_re, c_im)):
            block[k] = g[k] + change
            copies.append(pltpu.make_async_copy(block.at[k], green_out.at[0, 0, k], sems.at[k]))
            copies[k].start()
        for copy in copies:
            copy.wait()


def write_green(kernel, arrays, shape, given=None):
    vmem, hbm = (pl.BlockSpec(memory_space=space) for space in (pltpu.VMEM, pltpu.HBM))
    more = [] if given is None else [given]
    return pl.pallas_call(
        kernel,
        out_shape=jax.ShapeDtypeStruct(shape, f32),
        in_specs=[vmem] * len(arrays) + [hbm] * len(more),
        out_specs=hbm,
        scratch_shapes=[pltpu.VMEM(shape[2:], f32), pltpu.SemaphoreType.DMA((2,))],
        input_output_aliases={len(arrays): 0} if more else {},
        compiler_params=pltpu.CompilerParams(vmem_limit_bytes=40 * 2**20),
    )(*arrays, *more)


def call(kernel, outs, *arrays):
    vmem = pl.BlockSpec(memory_space=pltpu.VMEM)
    return pl.pallas_call(
        kernel,
        out_shape=[jax.ShapeDtypeStruct(shape, f32) for shape in outs],
        in_specs=[vmem] * len(arrays),
        out_specs=[vmem] * len(outs),
        compiler_params=pltpu.CompilerParams(vmem_limit_bytes=40 * 2**20),
    )(*arrays)


def exchange(energies, hamiltonian, coupling, green_prev, profile, phonon_weights, source, weight_index, left_face):
    count = lax.axis_size("energy")
    width = green_prev.shape[-1]
    block = (width, width)
    all_twin, all_x = pairs_of(twin, count), pairs_of(over_x, count)
    all_1, all_2 = pairs_of(group_1, count), pairs_of(group_2, count)
    groups = count // 4
    near_pairs = [(4 * k, 4 * k - 1) for k in range(2, groups)] + [(4 * k + 3, 4 * k + 4) for k in range(groups - 2)]
    far_pairs = [p for k in range(1, groups - 1) for p in ((4 * k, 4 * k - 1), (4 * k + 3, 4 * k + 4))]
    pair = sent(green_prev, all_twin)
    im, re = pack(green_prev, energies, source, weight_index, phonon_weights)
    x = sent(im, all_x)
    one = sent(re, all_1)
    two = sent(re, all_2)
    near = sent(im, near_pairs)
    x, near = lax.optimization_barrier((x, near))
    pair_one = sent(one, all_twin)
    pair_two = sent(two, all_twin)
    pair_x = sent(x, all_twin)
    (over_x_sum,) = call(over_x_kernel, [block], re, pair, one, two, pair_one, pair_two, x)
    sum_1, sum_2 = call(
        groups_kernel, [block] * 2, im, pair, x, pair_x, near, one, two
    )
    two_later, sum_1, sum_2, over_x_sum = lax.optimization_barrier((two, sum_1, sum_2, over_x_sum))
    from_x = sent(over_x_sum, all_x)
    from_1 = sent(sum_1, all_1)
    from_2 = sent(sum_2, all_2)
    far = sent(two_later, far_pairs)
    own, placed = call(
        own_kernel, [(2, *block), (width, coupling.shape[1])],
        re, im, pair, one, two, pair_one, pair_two, x, pair_x, hamiltonian, profile, coupling, left_face,
    )
    return placed, (own, re, profile, from_x, far, from_1, from_2)


def passed_along(value, steps):
    count = lax.axis_size("slab")
    return lax.ppermute(value, "slab", [(start, (start + steps) % count) for start in range(count)])


def on_device(
    energies, hamiltonian, coupling, green_prev, profile, phonon_weights, source, weight_index, left_face, right_face,
):
    width, faces = hamiltonian.shape[1], coupling.shape[1]
    slabs = lax.axis_size("slab")
    block, face = (width, width), (faces, 2 * faces)
    parts_of_g = [(2, *block), (2 * width, faces), (faces, 2 * width)]
    placed, parts = exchange(
        energies, hamiltonian, coupling, green_prev, profile, phonon_weights, source, weight_index, left_face
    )
    face_sent, base = call(first_kernel, [face, (2, *block)], *parts, right_face)
    incoming = passed_along(face_sent, 1)
    for turn in range(1, slabs - 1):
        (face_sent,) = call(face_kernel, [face], base, placed, incoming, right_face)
        incoming = passed_along(face_sent, 1)
    g, cols, rows = call(slab_0_kernel, parts_of_g, base, right_face)
    placed, g = lax.optimization_barrier((placed, g))
    if slabs > 2:
        g, cols, rows = call(
            functools.partial(middle_kernel, slabs), parts_of_g, base, placed, incoming, right_face, g, cols, rows
        )
    message, series, scaled = call(
        functools.partial(turn_kernel, slabs), [face, (DOUBLINGS, *block), (2, *block)], base, placed, incoming
    )
    incoming = passed_along(message, -1)
    green = write_green(functools.partial(last_full_kernel, slabs), [series, scaled], green_prev.shape)
    for turn in range(2, slabs):
        (message,) = call(
            functools.partial(message_kernel, slabs), [face],
            cols, incoming, message, coupling, left_face, right_face, base,
        )
        incoming = passed_along(message, -1)
    return write_green(functools.partial(last_kernel, slabs), [g, cols, rows, incoming], green_prev.shape, green)


def solution(mesh):
    in_specs = (
        P("energy"),
        P("slab", None, None),
        P("slab", None, None),
        P("energy", "slab", None, None, None),
        P(),
        P(),
        P("energy", None),
        P("energy", None),
        P("slab", None),
        P("slab", None),
    )
    out_specs = P("energy", "slab", None, None, None)
    return jax.shard_map(on_device, mesh=mesh, in_specs=in_specs, out_specs=out_specs, check_vma=False)
```

```python
import functools

import jax
import jax.numpy as jnp
from jax import lax
from jax.experimental import pallas as pl
from jax.experimental.pallas import tpu as pltpu
from jax.sharding import PartitionSpec as P

SPAN = 5
BROAD = 0.02
DOUBLINGS = 4

f32 = jnp.float32
bf16 = jnp.bfloat16
NN = (((1,), (0,)), ((), ()))
NT = (((1,), (1,)), ((), ()))
TN = (((0,), (0,)), ((), ()))


def split(x):
    high = x.astype(bf16)
    return high, (x - high.astype(f32)).astype(bf16)


def mm(a, b, dims=NN):
    return lax.dot_general(a, b, dims, preferred_element_type=f32)


def left3(*terms):
    out = []
    for x in terms:
        high, low = split(x)
        out += [high, high, low]
    return jnp.concatenate(out, axis=1)


def right3(*terms, axis=0):
    out = []
    for x in terms:
        high, low = split(x)
        out += [high, low, high]
    return jnp.concatenate(out, axis=axis)


def pair(x, axis):
    return jnp.concatenate(split(x), axis=axis)


def twice(x, axis):
    return jnp.concatenate([x, x], axis=axis)


def both(x_re, x_im):
    return jnp.concatenate([x_re, x_im], axis=0)


def skew(e):
    return 0.5 * (e - e.T)


def stack(*parts):
    return jnp.concatenate(parts, axis=0)


def left_of(high, low):
    return jnp.concatenate([high, high, low], axis=1)


def right_of(high, low):
    return jnp.concatenate([high, low, high], axis=0)


def herm(e, q):
    return split(e), split(q)


def times(s, h):
    return mm(left_of(*s[0]), right_of(*h[0])) - 2.0 * mm(left_of(*s[1]), right_of(*h[1]))


def rows_times(e_rows, q_rows, h):
    count = e_rows.shape[0]
    e_high, e_low = split(e_rows)
    q_high, q_low = split(q_rows)
    from_e = mm(stack(e_high, e_low), h[0][0])
    from_q = mm(stack(q_high, q_low), h[1][0])
    lows = mm(e_high, h[0][1]) + mm(q_high, h[1][1])
    return (from_e[:count] + from_e[count:]) + (from_q[:count] + from_q[count:]) + lows


def thin_times(y_re, y_im, h):
    out = rows_times(stack(y_re, y_im), stack(-(y_re + y_im), y_re - y_im), h)
    return out[:y_re.shape[0]], out[y_re.shape[0]:]


def complex_mm(a_re, a_im, b_re, b_im):
    rows = a_re.shape[0]
    out = mm(stack(left3(a_re, -a_im), left3(a_im, a_re)), right3(b_re, b_im))
    return out[:rows], out[rows:]


def one_hot(width, face):
    return (lax.broadcasted_iota(jnp.int32, (width, face.shape[1]), 0) == face).astype(bf16)


def unit_of(width):
    row = lax.broadcasted_iota(jnp.int32, (width, width), 0)
    return (row == lax.broadcasted_iota(jnp.int32, (width, width), 1)).astype(f32)


def begin(a_re, a_im):
    total = a_re + a_im
    gram = mm(left3(total), right3(total, axis=1), NT) - mm(left3(2.0 * a_re), right3(a_im, axis=1), NT)
    modulus = jnp.sqrt(a_re * a_re + a_im * a_im)
    col_norm = jnp.max(jnp.sum(modulus, axis=0))
    row_norm = jnp.max(jnp.sum(modulus, axis=1))
    scale = 1.0 / (col_norm * row_norm)
    return unit_of(a_re.shape[0]) - scale * gram, (-scale) * skew(gram), scale


def corner(a_re, a_im, proj):
    width, faces = proj.shape
    e, q, scale = begin(a_re, a_im)
    proj_t = proj.T
    y = scale * mm(left3(proj_t), right3(both(a_re, a_im), axis=1), NT)
    y_re, y_im = y[:, :width], -y[:, width:]
    powers = [e]
    for turn in range(1, DOUBLINGS):
        h = herm(e, q)
        e = times(h, h)
        q = skew(e)
        powers.append(e)
        c_re, c_im = thin_times(y_re, y_im, h)
        y_re, y_im = y_re + c_re, y_im + c_im
    h = herm(e, q)
    c_re, c_im = thin_times(y_re, y_im, h)
    y_re, y_im = y_re + c_re, y_im + c_im
    none = jnp.zeros_like(proj_t)
    t_re, t_im = thin_times(proj_t, none, h)
    u_re, u_im = thin_times(y_re, y_im, h)
    out = mm(left3(both(y_re, y_im)), right3(proj))
    out += mm(stack(left3(u_re, u_im), left3(u_im, -u_re)), right3(t_re, t_im, axis=1), NT)
    return out[:faces], out[faces:], powers, scale


def series_of(e, q):
    s_e, s_q = unit_of(e.shape[0]) + e, q
    for turn in range(1, DOUBLINGS):
        h = herm(e, q)
        if turn > 1:
            s_e = s_e + times(herm(s_e, s_q), h)
            s_q = skew(s_e)
        e = times(h, h)
        q = skew(e)
    return s_e, s_q, e, q


def full(a_re, a_im, s_e, s_q, e, q, store):
    h = herm(e, q)
    s_e = s_e + times(herm(s_e, s_q), h)
    e = times(h, h)
    s_e = s_e + times(herm(s_e, skew(s_e)), herm(e, skew(e)))
    s_q = skew(s_e)
    s_p = s_e - s_q
    b, c = a_re.T, a_im.T
    one = mm(left3(b - c), right3(s_p))
    store(0, one + mm(left3(c), right3(s_e)))
    store(1, one + mm(left3(b), right3(s_q - s_p)))


ROWS = 8


def over_x(e):
    return e ^ 2


def twin(e):
    return e ^ 1


def group_1(e):
    return e + 4 if e % 2 == 0 else e - 4


def group_2(e):
    return e - 4 if e % 2 == 0 else e + 4


def sent(value, pairs):
    return lax.ppermute(value, "energy", pairs)


def pairs_of(target, count):
    return [(e, target(e)) for e in range(count) if 0 <= target(e) < count]


def pack_kernel(energy_hbm, source_hbm, index_hbm, table_hbm, green, im_out, re_out, energy, source, index, table, sems):
    width = green.shape[3]
    copies = [
        pltpu.make_async_copy(start, end, sems.at[k])
        for k, (start, end) in enumerate((
            (energy_hbm, energy), (source_hbm, source), (index_hbm, index), (table_hbm, table),
            (green.at[0, 0, 1], im_out.at[pl.ds(0, width)]), (green.at[0, 0, 0], re_out.at[pl.ds(0, width)]),
        ))
    ]
    for copy in copies:
        copy.start()
    for copy in copies[:4]:
        copy.wait()
    row = lax.broadcasted_iota(jnp.int32, (ROWS, width), 0)
    rows = jnp.where(row == 4, energy[0], 0.0)
    for term in range(2):
        rows = jnp.where(row == term, source[0, term].astype(f32), rows)
        rows = jnp.where(row == 2 + term, table[index[0, term]], rows)
    im_out[width:] = rows
    re_out[width:] = rows
    for copy in copies[4:]:
        copy.wait()


def pack(green_prev, energies, source, weight_index, table):
    width = green_prev.shape[-1]
    hbm, vmem = pl.BlockSpec(memory_space=pltpu.HBM), pl.BlockSpec(memory_space=pltpu.VMEM)
    return pl.pallas_call(
        pack_kernel,
        out_shape=[jax.ShapeDtypeStruct((width + ROWS, width), f32)] * 2,
        in_specs=[hbm] * 5,
        out_specs=[vmem] * 2,
        scratch_shapes=[
            pltpu.SMEM(energies.shape, f32), pltpu.SMEM(source.shape, jnp.int32),
            pltpu.SMEM(weight_index.shape, jnp.int32), pltpu.SMEM(table.shape, f32),
            pltpu.SemaphoreType.DMA((6,)),
        ],
        compiler_params=pltpu.CompilerParams(vmem_limit_bytes=40 * 2**20),
    )(energies, source, weight_index, table, pltpu.with_memory_space_constraint(green_prev, pltpu.HBM))


def coef(rows, index):
    at = index.astype(f32)
    return jnp.where(rows[0:1] == at, rows[2:3], 0.0) + jnp.where(rows[1:2] == at, rows[3:4], 0.0)


def held(e):
    step = jnp.where(e % 2 == 0, 4, -4)
    other = e + 1 - 2 * (e % 2)
    return other, e - step, e + step, other + step, other - step


def over_x_kernel(re, twin_block, one, two, pair_one, pair_two, x, out):
    width = re.shape[1]
    e = lax.axis_index("energy")
    other, at_one, at_two, at_pair_one, at_pair_two = held(e)
    rows = x[width:]
    total = coef(rows, e) * re[:width] + coef(rows, other) * twin_block[0, 0, 0]
    total += coef(rows, at_one) * one[:width] + coef(rows, at_two) * two[:width]
    out[...] = total + coef(rows, at_pair_one) * pair_one[:width] + coef(rows, at_pair_two) * pair_two[:width]


def groups_kernel(im, twin_block, x, pair_x, near, one, two, out_1, out_2):
    width = im.shape[1]
    e = lax.axis_index("energy")
    other, at_one, at_two, _, _ = held(e)
    across = e + 2 - 4 * ((e // 2) % 2)
    pair_across = other + 2 - 4 * ((other // 2) % 2)
    for target, rows, out in ((at_two, two[width:], out_1), (at_one, one[width:], out_2)):
        upward = target > e
        near_index = jnp.where(upward, e - 1, e + 1)
        counts = e % 4 == jnp.where(upward, 0, 3)
        total = coef(rows, e) * im[:width] + coef(rows, other) * twin_block[0, 0, 1]
        total += coef(rows, across) * x[:width] + coef(rows, pair_across) * pair_x[:width]
        out[...] = total + jnp.where(counts, coef(rows, near_index), 0.0) * near[:width]


def own_kernel(re, im, twin_block, one, two, pair_one, pair_two, x, pair_x, ham, profile, coup, left, base_out, placed_out):
    width = re.shape[1]
    e = lax.axis_index("energy")
    other, at_one, at_two, at_pair_one, at_pair_two = held(e)
    across = e + 2 - 4 * ((e // 2) % 2)
    pair_across = other + 2 - 4 * ((other // 2) % 2)
    rows = re[width:]
    total = coef(rows, e) * re[:width] + coef(rows, other) * twin_block[0, 0, 0]
    total += coef(rows, at_one) * one[:width] + coef(rows, at_two) * two[:width]
    total += coef(rows, at_pair_one) * pair_one[:width] + coef(rows, at_pair_two) * pair_two[:width]
    unit = unit_of(width)
    base_out[0] = rows[4:5] * unit - ham[0] - profile[...] * total
    total = coef(rows, e) * im[:width] + coef(rows, other) * twin_block[0, 0, 1]
    total += coef(rows, across) * x[:width] + coef(rows, pair_across) * pair_x[:width]
    placed = mm(twice(one_hot(width, left[...]), 1), pair(coup[0], 1), NT)
    placed_out[...] = placed
    lead = jnp.where(lax.axis_index("slab") == 0, -0.5, 0.0) * mm(left3(placed), right3(placed, axis=1), NT)
    base_out[1] = BROAD * unit - profile[...] * total - lead


def first_kernel(own, re, profile, from_x, far, from_1, from_2, right, face_out, base_out):
    width, faces = profile.shape[0], right.shape[1]
    e = lax.axis_index("energy")
    weight = coef(re[width:], jnp.where(e % 4 == 3, e + SPAN, e - SPAN))
    base_re = own[0] - profile[...] * (from_x[...] + weight * far[:width])
    base_im = own[1] - profile[...] * (from_1[...] + from_2[...])
    base_out[0] = base_re
    base_out[1] = base_im

    @pl.when(lax.axis_index("slab") == 0)
    def _():
        f_re, f_im, _, _ = corner(base_re, base_im, one_hot(width, right[...]).astype(f32))
        face_out[:, :faces] = f_re
        face_out[:, faces:] = f_im


def bounded(base, placed, incoming):
    width, faces = placed.shape
    is_first = lax.axis_index("slab") == 0
    face = jnp.where(is_first, 0.0, incoming[...])
    split_placed = left3(placed[...])
    t = mm(split_placed, right3(face))
    bound = mm(stack(left3(t[:, :faces]), left3(t[:, faces:])), right3(placed[...], axis=1), NT)
    return base[0] - bound[:width], base[1] - bound[width:]


def face_kernel(base, placed, incoming, right, face_out):
    width, faces = placed.shape
    a_re, a_im = bounded(base, placed, incoming)
    f_re, f_im, _, _ = corner(a_re, a_im, one_hot(width, right[...]).astype(f32))
    face_out[:, :faces] = f_re
    face_out[:, faces:] = f_im


def face_parts(g_re, g_im, right, cols_out, rows_out):
    width = g_re.shape[0]
    hot = one_hot(width, right[...])
    high, low = split(both(g_re, g_im))
    cols_out[...] = mm(jnp.concatenate([high, low], axis=1), twice(hot, 0))
    wide_high = jnp.concatenate([high[:width], high[width:]], axis=1)
    wide_low = jnp.concatenate([low[:width], low[width:]], axis=1)
    rows_out[...] = mm(twice(hot.T, 1), stack(wide_high, wide_low))


def whole(a_re, a_im, right, g_out, cols_out, rows_out):
    e, q, scale = begin(a_re, a_im)

    def store(k, part):
        g_out[k] = part

    full(scale * a_re, scale * a_im, *series_of(e, q), store)
    face_parts(g_out[0], g_out[1], right, cols_out, rows_out)


def slab_0_kernel(base, right, g_out, cols_out, rows_out):
    @pl.when(lax.axis_index("slab") == 0)
    def _():
        whole(base[0], base[1], right, g_out, cols_out, rows_out)


def middle_kernel(slabs, base, placed, incoming, right, g, cols, rows, g_out, cols_out, rows_out):
    slab = lax.axis_index("slab")

    @pl.when((slab != 0) & (slab != slabs - 1))
    def _():
        a_re, a_im = bounded(base, placed, incoming)
        whole(a_re, a_im, right, g_out, cols_out, rows_out)

    @pl.when((slab == 0) | (slab == slabs - 1))
    def _():
        g_out[...] = g[...]
        cols_out[...] = cols[...]
        rows_out[...] = rows[...]


def turn_kernel(slabs, base, placed, incoming, message_out, series_out, a_out):
    @pl.when(lax.axis_index("slab") == slabs - 1)
    def _():
        width, faces = placed.shape
        a_re, a_im = bounded(base, placed, incoming)
        m_re, m_im, series, scale = corner(a_re, a_im, placed[...])
        message_out[:, :faces] = m_re
        message_out[:, faces:] = m_im
        for k, part in enumerate(series):
            series_out[k] = part
        a_out[0] = scale * a_re
        a_out[1] = scale * a_im


def message_kernel(slabs, cols, message, own, coup, left, right, base, message_out):
    width, faces = base.shape[1], coup.shape[1]
    hot = one_hot(width, right[...])
    f = mm(twice(hot.T, 1), pair(cols[:width], 0))
    f_im = mm(twice(hot.T, 1), pair(cols[width:], 0))
    order = mm(one_hot(width, left[...]), hot, TN).astype(bf16)
    mixed = mm(pair(coup[0], 1), twice(order, 0))
    t_re, t_im = complex_mm(f, f_im, message[:, :faces], message[:, faces:])
    c_re, c_im = complex_mm(t_re, t_im, f, f_im)
    t = mm(left3(both(f + c_re, f_im + c_im)), right3(mixed, axis=1), NT)
    wide = jnp.concatenate([t[:faces], t[faces:]], axis=1)
    is_last = lax.axis_index("slab") == slabs - 1

    @pl.when(jnp.logical_not(is_last))
    def _():
        message_out[...] = mm(left3(mixed), right3(wide))

    @pl.when(is_last)
    def _():
        message_out[...] = own[...]


def last_full_kernel(slabs, series, scaled, green_out, block, sems):
    @pl.when(lax.axis_index("slab") == slabs - 1)
    def _():
        e, s_e = series[0], unit_of(scaled.shape[1]) + series[0]
        for turn in range(1, DOUBLINGS - 1):
            e = series[turn]
            s_e = s_e + times(herm(s_e, skew(s_e)), herm(e, skew(e)))
        e = series[DOUBLINGS - 1]
        copies = [pltpu.make_async_copy(block.at[k], green_out.at[0, 0, k], sems.at[k]) for k in range(2)]

        def store(k, part):
            block[k] = part
            copies[k].start()

        full(scaled[0], scaled[1], s_e, skew(s_e), e, skew(e), store)
        for copy in copies:
            copy.wait()


def last_kernel(slabs, g, cols, rows, message, given, green_out, block, sems):
    @pl.when(lax.axis_index("slab") != slabs - 1)
    def _():
        width, faces = g.shape[1], message.shape[0]
        t_re, t_im = complex_mm(message[:, :faces], message[:, faces:], rows[:, :width], rows[:, width:])
        half = width // 2
        copies = []
        for at in (0, half):
            rows_at = pl.ds(at, half)
            changes = complex_mm(cols[at:at + half], cols[width + at:width + at + half], t_re, t_im)
            for k, change in enumerate(changes):
                block[k, rows_at] = g[k, rows_at] + change
                copies.append(pltpu.make_async_copy(
                    block.at[k, rows_at], green_out.at[0, 0, k, rows_at], sems.at[len(copies)]
                ))
                copies[-1].start()
        for copy in copies:
            copy.wait()


def write_green(kernel, arrays, shape, given=None):
    vmem, hbm = (pl.BlockSpec(memory_space=space) for space in (pltpu.VMEM, pltpu.HBM))
    more = [] if given is None else [given]
    return pl.pallas_call(
        kernel,
        out_shape=jax.ShapeDtypeStruct(shape, f32),
        in_specs=[vmem] * len(arrays) + [hbm] * len(more),
        out_specs=hbm,
        scratch_shapes=[pltpu.VMEM(shape[2:], f32), pltpu.SemaphoreType.DMA((4,))],
        input_output_aliases={len(arrays): 0} if more else {},
        compiler_params=pltpu.CompilerParams(vmem_limit_bytes=40 * 2**20),
    )(*arrays, *more)


def call(kernel, outs, *arrays):
    vmem = pl.BlockSpec(memory_space=pltpu.VMEM)
    return pl.pallas_call(
        kernel,
        out_shape=[jax.ShapeDtypeStruct(shape, f32) for shape in outs],
        in_specs=[vmem] * len(arrays),
        out_specs=[vmem] * len(outs),
        compiler_params=pltpu.CompilerParams(vmem_limit_bytes=40 * 2**20),
    )(*arrays)


def exchange(energies, hamiltonian, coupling, green_prev, profile, phonon_weights, source, weight_index, left_face):
    count = lax.axis_size("energy")
    width = green_prev.shape[-1]
    block = (width, width)
    all_twin, all_x = pairs_of(twin, count), pairs_of(over_x, count)
    all_1, all_2 = pairs_of(group_1, count), pairs_of(group_2, count)
    groups = count // 4
    near_pairs = [(4 * k, 4 * k - 1) for k in range(2, groups)] + [(4 * k + 3, 4 * k + 4) for k in range(groups - 2)]
    far_pairs = [p for k in range(1, groups - 1) for p in ((4 * k, 4 * k - 1), (4 * k + 3, 4 * k + 4))]
    pair = sent(green_prev, all_twin)
    im, re = pack(green_prev, energies, source, weight_index, phonon_weights)
    x = sent(im, all_x)
    one = sent(re, all_1)
    two = sent(re, all_2)
    near = sent(im, near_pairs)
    x, near = lax.optimization_barrier((x, near))
    pair_one = sent(one, all_twin)
    pair_two = sent(two, all_twin)
    pair_x = sent(x, all_twin)
    (over_x_sum,) = call(over_x_kernel, [block], re, pair, one, two, pair_one, pair_two, x)
    sum_1, sum_2 = call(
        groups_kernel, [block] * 2, im, pair, x, pair_x, near, one, two
    )
    two_later, sum_1, sum_2, over_x_sum = lax.optimization_barrier((two, sum_1, sum_2, over_x_sum))
    from_x = sent(over_x_sum, all_x)
    from_1 = sent(sum_1, all_1)
    from_2 = sent(sum_2, all_2)
    far = sent(two_later, far_pairs)
    own, placed = call(
        own_kernel, [(2, *block), (width, coupling.shape[1])],
        re, im, pair, one, two, pair_one, pair_two, x, pair_x, hamiltonian, profile, coupling, left_face,
    )
    return placed, (own, re, profile, from_x, far, from_1, from_2)


def passed_along(value, steps):
    count = lax.axis_size("slab")
    return lax.ppermute(value, "slab", [(start, (start + steps) % count) for start in range(count)])


def on_device(
    energies, hamiltonian, coupling, green_prev, profile, phonon_weights, source, weight_index, left_face, right_face,
):
    width, faces = hamiltonian.shape[1], coupling.shape[1]
    slabs = lax.axis_size("slab")
    block, face = (width, width), (faces, 2 * faces)
    parts_of_g = [(2, *block), (2 * width, faces), (faces, 2 * width)]
    placed, parts = exchange(
        energies, hamiltonian, coupling, green_prev, profile, phonon_weights, source, weight_index, left_face
    )
    face_sent, base = call(first_kernel, [face, (2, *block)], *parts, right_face)
    incoming = passed_along(face_sent, 1)
    for turn in range(1, slabs - 1):
        (face_sent,) = call(face_kernel, [face], base, placed, incoming, right_face)
        incoming = passed_along(face_sent, 1)
    g, cols, rows = call(slab_0_kernel, parts_of_g, base, right_face)
    placed, g = lax.optimization_barrier((placed, g))
    if slabs > 2:
        g, cols, rows = call(
            functools.partial(middle_kernel, slabs), parts_of_g, base, placed, incoming, right_face, g, cols, rows
        )
    message, series, scaled = call(
        functools.partial(turn_kernel, slabs), [face, (DOUBLINGS, *block), (2, *block)], base, placed, incoming
    )
    incoming = passed_along(message, -1)
    green = write_green(functools.partial(last_full_kernel, slabs), [series, scaled], green_prev.shape)
    for turn in range(2, slabs):
        (message,) = call(
            functools.partial(message_kernel, slabs), [face],
            cols, incoming, message, coupling, left_face, right_face, base,
        )
        incoming = passed_along(message, -1)
    return write_green(functools.partial(last_kernel, slabs), [g, cols, rows, incoming], green_prev.shape, green)


def solution(mesh):
    in_specs = (
        P("energy"),
        P("slab", None, None),
        P("slab", None, None),
        P("energy", "slab", None, None, None),
        P(),
        P(),
        P("energy", None),
        P("energy", None),
        P("slab", None),
        P("slab", None),
    )
    out_specs = P("energy", "slab", None, None, None)
    return jax.shard_map(on_device, mesh=mesh, in_specs=in_specs, out_specs=out_specs, check_vma=False)
```
